128 devices in a mesh: face: 8 (over z, core), blk: 16 (over x, y).
Axes of the slice: x: 4, y: 4, z: 4, core: 2. Of those that a mesh axis runs over, the one named last changes fastest.
Arguments:
- fields: float32 [1024, 96, 2048], P('face', None, 'blk'), may hold values from -6 to 6
- weights: bfloat16 [128, 16, 8, 384, 128], P(('face', 'blk')), may hold values from -0.21875 to 0.21875
- src_tile: int32 [128, 16, 8], P(('face', 'blk')), may hold values from 0 to 127
- tgt_tile: int32 [128, 16, 8], P(('face', 'blk')), may hold values from 0 to 15, as said below
- counts: int32 [128, 16], P(('face', 'blk')), may hold values from 0 to 8, as said below
Outputs:
- remapped: float32 [2048, 96, 128], P(('face', 'blk'))
The draws below stay inside these ranges and needn't reach their ends.
Inputs may be any that keep to these rules, and one draw needn't show every extreme that they name: `tgt_tile`: the 8 slots of one source block toward one device name distinct target tiles. `counts`: every source block has all 8 slots live toward at least one device; blocks of the first and last row of blocks have at least 4 live slots toward every device.
All inputs are finite; a program needn't handle non-finite values.
Results may differ from the reference program's by a relative error of at most 0.009.
Values may be sent and summed in bfloat16 or wider, within the bound.
A program may use at most 128 MiB of HBM per device.

```python
import jax
import jax.numpy as jnp
from jax import lax

ROWS = 96
BX = 128
BY = 128
TC = 128
TPD = 16
C = 8
GX = 1024
GY = 2048
N_FACE = 8
N_BLK = 16


def draw_tgt_tile(key, part):
    key = jax.random.fold_in(key, 11)
    scores = jax.random.randint(key, (N_FACE * N_BLK, N_BLK, TPD), 0, 1 << 20)
    scores = scores * TPD + lax.broadcasted_iota(jnp.int32, (N_FACE * N_BLK, N_BLK, TPD), 2)
    order = jnp.argsort(scores, axis=-1)
    return order[:, :, :C].astype(jnp.int32)


def draw_counts(key, part):
    key = jax.random.fold_in(key, 23)
    first_key, second_key = jax.random.split(key)
    base = jax.random.randint(first_key, (N_FACE * N_BLK, N_BLK), 0, C + 1)
    face_row = lax.broadcasted_iota(jnp.int32, (N_FACE * N_BLK, N_BLK), 0) // N_BLK
    polar = jnp.logical_or(face_row == 0, face_row == N_FACE - 1)
    base = jnp.where(polar, jnp.maximum(base, C // 2), base)
    full_at = jax.random.randint(second_key, (N_FACE * N_BLK,), 0, N_BLK)
    writer_ids = lax.broadcasted_iota(jnp.int32, (N_FACE * N_BLK, N_BLK), 1)
    return jnp.where(writer_ids == full_at[:, None], C, base).astype(jnp.int32)


def plant(values, rng, smallest, high):
    longest = values.shape.index(max(values.shape))
    spots = []
    for shift in (0, 1):
        where = [jax.random.randint(jax.random.fold_in(rng, axis), (), 0, length) for axis, length in enumerate(values.shape)]
        where[longest] = (where[longest] + shift) % values.shape[longest]
        spots.append(tuple(where))
    return values.at[spots[0]].set(smallest).at[spots[1]].set(high)


def level_of(stream_key, dims, pieces, least, high):
    def one(position, blocks):
        heights = jax.random.uniform(jax.random.fold_in(jax.random.fold_in(stream_key, 6), position), (blocks,), jnp.float32, least / len(pieces), high / len(pieces))
        return jnp.repeat(jnp.exp(heights), dims[position] // blocks).reshape((-1,) + (1,) * (len(dims) - position - 1))

    level = one(*pieces[0])
    for cut in pieces[1:]:
        level = level * one(*cut)
    return level


def centred(rng, dims, width, limit, shards=(), kind=jnp.bfloat16):
    drawn = jax.random.normal(rng, dims, jnp.float32) * width
    if len(shards) > 0:
        drawn = level_of(rng, dims, shards, -0.22, 0.18) * drawn
    return jnp.clip(drawn, min=-limit, max=limit).astype(kind)


def setup_inputs(seed: int = 0) -> dict:
    arg_keys = jax.random.split(jax.random.key(seed), 6)
    return {
        "fields": centred(arg_keys[0], (GX, ROWS, GY), 1.0, 6.0, ((0, 8), (2, 16)), jnp.float32),
        "weights": centred(arg_keys[1], (N_FACE * N_BLK, N_BLK, C, 3 * BY, TC), (3 * BY * 2) ** -0.5, 0.21875, ((0, 128),)),
        "src_tile": plant(jax.random.randint(arg_keys[2], (N_FACE * N_BLK, N_BLK, C), 0, BX), jax.random.fold_in(arg_keys[2], 1), 0, BX - 1).astype(jnp.int32),
        "tgt_tile": draw_tgt_tile(jax.random.fold_in(arg_keys[5], 71), 0),
        "counts": draw_counts(jax.random.fold_in(arg_keys[5], 71), 0),
    }


def reference(fields, weights, src_tile, tgt_tile, counts):
    grad_x = (jnp.roll(fields, -1, 0) - jnp.roll(fields, 1, 0)) * 0.5
    grad_y = (jnp.roll(fields, -1, 2) - jnp.roll(fields, 1, 2)) * 0.5
    joined = jnp.concatenate([
        fields.reshape(N_FACE, BX, ROWS, N_BLK, BY),
        grad_x.reshape(N_FACE, BX, ROWS, N_BLK, BY),
        grad_y.reshape(N_FACE, BX, ROWS, N_BLK, BY)], axis=4).astype(jnp.bfloat16)
    blocks = jnp.transpose(joined, (0, 3, 1, 2, 4)).reshape(N_FACE * N_BLK, BX, ROWS, 3 * BY)
    total = jnp.zeros((N_FACE, N_BLK, TPD, ROWS, TC), jnp.float32)

    def one_block(sender, total):
        block_rows = blocks[sender]
        picked = src_tile[sender].reshape(-1)
        chosen = jnp.take(block_rows, picked, axis=0).astype(jnp.float32)
        block_w = weights[sender].reshape(N_BLK * C, 3 * BY, TC).astype(jnp.float32)
        products = jnp.einsum('pmk,pkn->pmn', chosen, block_w)
        slot_ids = lax.broadcasted_iota(jnp.int32, (N_BLK, C), 1)
        live_mask = (slot_ids < counts[sender][:, None]).reshape(-1)
        partial_value = jnp.where(live_mask[:, None, None], products, 0.0).astype(jnp.bfloat16)
        one_hot = (tgt_tile[sender][:, :, None] == lax.broadcasted_iota(jnp.int32, (N_BLK, C, TPD), 2)).astype(jnp.float32)
        dense_tiles = jnp.einsum('dct,dcmn->dtmn', one_hot, partial_value.reshape(N_BLK, C, ROWS, TC).astype(jnp.float32))
        face_row = (sender // N_BLK).astype(jnp.int32)
        return total.at[face_row].add(dense_tiles)

    total = lax.fori_loop(0, N_FACE * N_BLK, one_block, total)
    return total.reshape(N_FACE * N_BLK * TPD, ROWS, TC)
```

```python
import jax
import jax.numpy as jnp
from jax import lax
from jax.experimental import pallas as pl
from jax.experimental.pallas import tpu as pltpu
from jax.sharding import PartitionSpec as P

MESH = pl.DeviceIdType.MESH
SIDE = 4
CHUNKS = 8
ROUTES = 2
PARTS = 2
STEPS = {"x+": (1, 0), "x-": (3, 0), "y+": (0, 1), "y-": (0, 3)}
TREES = (
    {
        (0, 1): "x-", (0, 2): "y+", (0, 3): "y+", (1, 0): "x-", (1, 1): "y+",
        (1, 2): "y+", (1, 3): "x-", (2, 0): "x+", (2, 1): "x+", (2, 2): "x-",
        (2, 3): "x-", (3, 0): "x+", (3, 1): "y-", (3, 2): "y-", (3, 3): "y+",
    },
    {
        (0, 1): "y-", (0, 2): "y-", (0, 3): "x+", (1, 0): "x-", (1, 1): "y-",
        (1, 2): "y+", (1, 3): "y+", (2, 0): "x-", (2, 1): "x+", (2, 2): "x+",
        (2, 3): "x-", (3, 0): "x+", (3, 1): "x+", (3, 2): "y-", (3, 3): "y-",
    },
)
PLAN = (
    ((3, 3), ()),
    ((2, 2), ()),
    ((2, 0), ()),
    ((1, 1), ()),
    ((2, 3), ()),
    ((0, 2), ()),
    ((2, 1), ()),
    ((3, 2), ((1, (3, 2), 0), (1, (3, 2), 1),)),
    ((1, 2), ((0, (1, 2), 0), (0, (1, 2), 1),)),
    ((0, 3), ()),
    ((0, 1), ()),
    ((1, 0), ()),
    ((3, 0), ()),
    ((0, 0), ()),
    ((3, 1), ()),
    ((1, 3), (
        (0, (1, 3), 0), (0, (3, 1), 0), (1, (1, 3), 0), (1, (3, 1), 0),
        (0, (3, 1), 1), (1, (1, 3), 1), (1, (3, 1), 1), (0, (1, 3), 1),
        (0, (0, 0), 0), (1, (0, 0), 0), (0, (3, 0), 0), (0, (0, 3), 0),
        (1, (0, 1), 0), (1, (1, 0), 0), (0, (3, 0), 1), (0, (0, 3), 1),
        (1, (0, 1), 1), (1, (1, 0), 1),
    )),
)
LAST = (
    (1, (0, 1), 0), (1, (1, 0), 0), (0, (0, 3), 0), (0, (3, 0), 0),
    (1, (0, 1), 1), (1, (1, 0), 1), (0, (0, 3), 1), (0, (3, 0), 1),
)
TABLES_AFTER = 6
ORDER = tuple(entry[0] for entry in PLAN)


def parent(route, o):
    dx, dy = STEPS[TREES[route][o]]
    return ((o[0] + dx) % SIDE, (o[1] + dy) % SIDE)


def children(route, o):
    return [v for v in TREES[route] if parent(route, v) == o]


INNER = [[v for v in tree if children(route, v)] for route, tree in enumerate(TREES)]
LEAVES = [[v for v in tree if not children(route, v)] for route, tree in enumerate(TREES)]


def coded(values):
    word = sum(v << (2 * k) for k, v in enumerate(values))
    return word - (1 << 32) if word >= 1 << 31 else word


def kernel(
    ints_in, fields_ref, weights_ref, out_ref,
    ints, cells, wts, part, col_own, col_send, col_recv, turns, tab_send, tab_recv, tab, sums, sums_in,
    *rest,
):
    raw_in = {}
    for route in range(ROUTES):
        for v in LEAVES[route]:
            raw_in[route, v] = rest[len(raw_in)]
    send_sem, recv_sem, field_sem, weight_sem, tab_sem, ints_sem = rest[len(raw_in):]
    bx, rows, width = fields_ref.shape
    cap, writers = ints.shape[1] // 2, ints.shape[2]
    tiles = out_ref.shape[0]
    height = rows // ROUTES
    share = tiles // PARTS
    faces = lax.axis_size("face")
    face = lax.axis_index("face")
    blk = lax.axis_index("blk")
    px, py = blk // SIDE, lax.rem(blk, SIDE)

    def at(a, b):
        return lax.rem(px + a, SIDE) * SIDE + lax.rem(py + b, SIDE)

    def writer(o):
        return at((SIDE - o[0]) % SIDE, (SIDE - o[1]) % SIDE)

    near = {name: (face, at(*step)) for name, step in STEPS.items()}
    up, down = lax.rem(face + 1, faces), lax.rem(face + faces - 1, faces)
    right, left = lax.rem(blk + 1, writers), lax.rem(blk + writers - 1, writers)
    barrier = pltpu.get_barrier_semaphore()
    greeted = [(up, blk), (down, blk), (face, left), (face, right)] + list(near.values())
    for peer in greeted:
        pl.semaphore_signal(barrier, inc=1, device_id=peer, device_id_type=MESH)

    fields_in = []
    step = bx // CHUNKS
    for i in range(CHUNKS):
        copy = pltpu.make_async_copy(
            fields_ref.at[pl.ds(i * step, step)], cells.at[pl.ds(1 + i * step, step)], field_sem.at[i]
        )
        copy.start()
        fields_in.append(copy)
    ints_copy = pltpu.make_async_copy(ints_in, ints, ints_sem)
    ints_copy.start()
    weights_in = [
        pltpu.make_async_copy(weights_ref.at[0, writer(o)], wts.at[k, :, pl.ds(0, weights_ref.shape[3])], weight_sem.at[k])
        for k, o in enumerate(ORDER)
    ]

    messages = []

    def message(src, dst, peer):
        i = len(messages)
        messages.append(
            pltpu.make_async_remote_copy(
                src_ref=src, dst_ref=dst, send_sem=send_sem.at[i], recv_sem=recv_sem.at[i],
                device_id=peer, device_id_type=MESH,
            )
        )
        return messages[i]

    halo = [
        message(fields_ref.at[bx - 1], cells.at[0], (up, blk)),
        message(fields_ref.at[0], cells.at[bx + 1], (down, blk)),
        message(col_send.at[0], col_recv.at[0], (face, right)),
        message(col_send.at[1], col_recv.at[1], (face, left)),
    ]
    tables = [message(tab_send, tab_recv.at[i], near[name]) for i, name in enumerate(STEPS)]
    raw, summed = {}, {}
    for route, tree in enumerate(TREES):
        rs = pl.ds(route * height, height)
        for v in LEAVES[route]:
            raw[route, v] = message(
                part.at[ORDER.index(v), pl.ds(0, cap), rs], raw_in[route, v].at[pl.ds(0, cap)], near[tree[v]]
            )
        for i, v in enumerate(INNER[route]):
            for h in range(PARTS):
                some = pl.ds(h * share, share)
                summed[route, v, h] = message(sums.at[route, i, some], sums_in.at[route, i, some], near[tree[v]])

    depth = weights_ref.shape[3]
    group = width // cap

    def clear(k, carry):
        for c in range(cap):
            wts[k, c, pl.ds(depth, width), :] = jnp.zeros((width, wts.shape[3]), wts.dtype)
        return carry

    lax.fori_loop(0, writers, clear, 0)

    pl.semaphore_wait(barrier, len(greeted))
    halo[0].start()
    halo[1].start()

    lanes = lax.broadcasted_iota(jnp.int32, (rows, width), 1)
    edges = (jnp.zeros((rows, width), jnp.float32), jnp.zeros((rows, width), jnp.float32))
    for i in range(CHUNKS):
        fields_in[i].wait()
        if i >= CHUNKS // 2:
            weights_in[i - CHUNKS // 2].start()

        def pick(j, edges):
            x = i * step + j
            turned = pltpu.roll(cells[1 + x], lax.rem(x + 1, width), 1)
            return (
                jnp.where(lanes == x, turned, edges[0]),
                jnp.where(lanes == lax.rem(x + 1, width), turned, edges[1]),
            )

        edges = lax.fori_loop(0, step, pick, edges, unroll=4)
    for i in range(2):
        col_own[i] = edges[i]
        col_send[i] = edges[i].astype(col_send.dtype)
    halo[2].start()
    halo[3].start()
    for copy in weights_in[CHUNKS - CHUNKS // 2:]:
        copy.start()

    ints_copy.wait()
    lane = lax.broadcasted_iota(jnp.int32, (1, 128), 1)

    def make_row(d, carry):
        row = jnp.full((1, 128), cap, jnp.int32)
        for c in range(cap):
            target = jnp.where(c < ints[0, 2 * cap, d], ints[0, cap + c, d], 127)
            row = jnp.where(lane == target, c, row)
        tab_send[pl.ds(d, 1), :] = row
        return carry

    lax.fori_loop(0, writers, make_row, 0)
    for copy in tables:
        copy.start()
    for buf in raw_in.values():
        buf[cap] = jnp.zeros((height, width), buf.dtype)
    for k, o in enumerate(ORDER):
        if o not in LEAVES[0] or o not in LEAVES[1]:
            part[k, cap] = jnp.zeros((rows, width), part.dtype)
    for copy in halo:
        copy.wait_recv()
    turns[:, pl.ds(0, width)] = (col_own[0] - col_recv[0].astype(jnp.float32)).astype(turns.dtype)
    turns[:, pl.ds(width, width)] = (col_recv[1].astype(jnp.float32) - col_own[1]).astype(turns.dtype)
    group_row = lax.broadcasted_iota(jnp.int32, (group, wts.shape[3]), 0)
    turn_row = lax.broadcasted_iota(jnp.int32, (2 * width, width), 0)

    def read_tables():
        for copy in tables:
            copy.wait_recv()
        sources = [tab_recv.at[i] for i in range(len(STEPS))] + [tab_send]
        copies = [pltpu.make_async_copy(src, tab.at[i], tab_sem.at[i]) for i, src in enumerate(sources)]
        for copy in copies:
            copy.start()
        for copy in copies:
            copy.wait()

    here = set()

    def gather(route, o, h, store):
        d = writer(o)
        k = ORDER.index(o)
        rs = pl.ds(route * height, height)
        below = children(route, o)
        plain = [v for v in below if v in LEAVES[route]]
        dense = [INNER[route].index(v) for v in below if v in INNER[route]]
        if o == (0, 0):
            dense = []
        for v in plain:
            if (route, v) not in here:
                raw[route, v].wait_recv()
                here.add((route, v))
        for i in dense:
            summed[route, INNER[route][i], h].wait_recv()
        ways = list(STEPS)

        def one(j, carry):
            t = h * share + j
            total = part[k, tab[len(ways), d, t], rs, :].astype(jnp.float32)
            for v in plain:
                slot = tab[ways.index(TREES[route][v]), d, t]
                total += raw_in[route, v][slot].astype(jnp.float32)
            for i in dense:
                total += sums_in[route, i, t].astype(jnp.float32)
            store(t, total)
            return carry

        lax.fori_loop(0, share, one, 0, unroll=4)

    def follow(route, o, h):
        if o == (0, 0):
            def store(t, total):
                out_ref[t, pl.ds(route * height, height), :] = total * 0.5

            for part_of in range(PARTS):
                gather(route, o, part_of, store)
        else:
            i = INNER[route].index(o)

            def store(t, total):
                sums[route, i, t] = total.astype(sums.dtype)

            gather(route, o, h, store)
            summed[route, o, h].start()

    code_x = jnp.int32(coded([(SIDE - o[0]) % SIDE for o in ORDER]))
    code_y = jnp.int32(coded([(SIDE - o[1]) % SIDE for o in ORDER]))

    def products(k, carry):
        d = at((code_x >> (2 * k)) & 3, (code_y >> (2 * k)) & 3)
        pltpu.make_async_copy(weights_ref.at[0, 0], wts.at[k, :, pl.ds(0, depth)], weight_sem.at[k]).wait()
        where_from = jnp.full((1, width), -1, jnp.int32)
        for c in range(cap):
            x = ints[0, c, d]
            where_from = jnp.where(lane == c * group, x, where_from)
            where_from = jnp.where(lane == c * group + group - 1, width + lax.rem(x + 1, width), where_from)
            first = wts[k, c, pl.ds(2 * width, group), :].astype(jnp.float32)
            final = wts[k, c, pl.ds(3 * width - group, group), :].astype(jnp.float32)
            edge = jnp.where(group_row == 0, first, jnp.where(group_row == group - 1, final, 0.0))
            wts[k, c, pl.ds(depth + c * group, group), :] = edge.astype(wts.dtype)
        chosen = jnp.where(turn_row == where_from, 1.0, 0.0).astype(jnp.bfloat16)
        turned = jnp.dot(turns[...], chosen, preferred_element_type=jnp.float32).astype(jnp.bfloat16)
        for c in range(cap):
            x = ints[0, c, d]
            value = cells[x + 1]
            grad_x = cells[x + 2] - cells[x]
            grad_y = pltpu.roll(value, width - 1, 1) - pltpu.roll(value, 1, 1)
            stacked = jnp.concatenate([value + value, grad_x, grad_y], axis=1).astype(jnp.bfloat16)
            stacked = jnp.concatenate([stacked, turned], axis=1)
            product = jnp.dot(stacked, wts[k, c], preferred_element_type=jnp.float32)
            part[k, c] = product.astype(part.dtype)

        for i, (o, sums_after) in enumerate(PLAN):
            ready = [raw[route, o] for route in range(ROUTES) if o in LEAVES[route]]
            if i == len(PLAN) - 1:
                sums_after = ()
            if ready or sums_after or i == TABLES_AFTER:
                @pl.when(k == i)
                def _():
                    for copy in ready:
                        copy.start()
                    if i == TABLES_AFTER:
                        read_tables()
                    for entry in sums_after:
                        follow(*entry)
        return carry

    lax.fori_loop(0, len(PLAN), products, 0)
    for entry in PLAN[-1][1]:
        follow(*entry)
    for route, v, h in LAST:
        rs = pl.ds(route * height, height)
        i = INNER[route].index(v)
        summed[route, v, h].wait_recv()

        def add(j, carry):
            t = h * share + j
            out_ref[t, rs, :] += sums_in[route, i, t].astype(jnp.float32) * 0.5
            return carry

        lax.fori_loop(0, share, add, 0, unroll=4)
    for copy in messages:
        copy.wait_send()


def on_device(fields, weights, src_tile, tgt_tile, counts):
    bx, rows, width = fields.shape
    _, writers, cap, depth, tile_cells = weights.shape
    tiles = 16
    height = rows // ROUTES
    leaves = sum(len(some) for some in LEAVES)
    inner = len(INNER[0])
    messages = 8 + leaves + ROUTES * inner * PARTS
    bf16 = jnp.bfloat16
    ints = jnp.concatenate(
        [jnp.swapaxes(src_tile, 1, 2), jnp.swapaxes(tgt_tile, 1, 2), counts[:, None, :]], axis=1
    )
    return pl.pallas_call(
        kernel,
        out_shape=jax.ShapeDtypeStruct((tiles, rows, tile_cells), jnp.float32),
        in_specs=[pl.BlockSpec(memory_space=pl.ANY)] * 3,
        out_specs=pl.BlockSpec(memory_space=pltpu.VMEM),
        scratch_shapes=[
            pltpu.SMEM((1, 2 * cap + 1, writers), jnp.int32),
            pltpu.VMEM((bx + 2, rows, width), jnp.float32),
            pltpu.VMEM((writers, cap, depth + width, tile_cells), bf16),
            pltpu.VMEM((writers, cap + 1, rows, tile_cells), bf16),
            pltpu.VMEM((2, rows, width), jnp.float32),
            pltpu.VMEM((2, rows, width), bf16),
            pltpu.VMEM((2, rows, width), bf16),
            pltpu.VMEM((rows, 2 * width), bf16),
            pltpu.VMEM((writers, 128), jnp.int32),
            pltpu.VMEM((len(STEPS), writers, 128), jnp.int32),
            pltpu.SMEM((len(STEPS) + 1, writers, 128), jnp.int32),
            pltpu.VMEM((ROUTES, inner, tiles, height, tile_cells), bf16),
            pltpu.VMEM((ROUTES, inner, tiles, height, tile_cells), bf16),
        ]
        + [pltpu.VMEM((cap + 1, height, tile_cells), bf16)] * leaves
        + [
            pltpu.SemaphoreType.DMA((messages,)),
            pltpu.SemaphoreType.DMA((messages,)),
            pltpu.SemaphoreType.DMA((CHUNKS,)),
            pltpu.SemaphoreType.DMA((writers,)),
            pltpu.SemaphoreType.DMA((len(STEPS) + 1,)),
            pltpu.SemaphoreType.DMA,
        ],
        compiler_params=pltpu.CompilerParams(
            collective_id=0, has_side_effects=True, vmem_limit_bytes=52 * 1024 * 1024
        ),
        cost_estimate=pl.CostEstimate(flops=1208000000, bytes_accessed=19700000, transcendentals=0),
    )(ints, fields, weights)


def solution(mesh):
    placed = (
        P("face", None, "blk"),
        P(("face", "blk"), None, None, None, None),
        P(("face", "blk"), None, None),
        P(("face", "blk"), None, None),
        P(("face", "blk"), None),
    )
    return jax.shard_map(
        on_device,
        mesh=mesh,
        in_specs=placed,
        out_specs=P(("face", "blk"), None, None),
        check_vma=False,
    )
```

```python
import jax
import jax.numpy as jnp
from jax import lax
from jax.experimental import pallas as pl
from jax.experimental.pallas import tpu as pltpu
from jax.sharding import PartitionSpec as P

MESH = pl.DeviceIdType.MESH
SIDE = 4
CHUNKS = 8
ROUTES = 2
PARTS = 2
STEPS = {"x+": (1, 0), "x-": (3, 0), "y+": (0, 1), "y-": (0, 3)}
TREES = (
    {
        (0, 1): "y-", (0, 2): "y+", (0, 3): "y+", (1, 0): "x-", (1, 1): "x-",
        (1, 2): "y-", (1, 3): "x-", (2, 0): "y+", (2, 1): "x-", (2, 2): "y-",
        (2, 3): "x+", (3, 0): "x+", (3, 1): "x+", (3, 2): "y+", (3, 3): "x+",
    },
    {
        (0, 1): "y-", (0, 2): "x+", (0, 3): "y+", (1, 0): "x-", (1, 1): "y-",
        (1, 2): "y-", (1, 3): "y+", (2, 0): "x+", (2, 1): "x-", (2, 2): "x-",
        (2, 3): "x+", (3, 0): "x+", (3, 1): "y-", (3, 2): "y+", (3, 3): "y+",
    },
)
PLAN = (
    ((2, 0), ()),
    ((2, 2), ()),
    ((0, 2), ()),
    ((2, 1), ()),
    ((3, 1), ()),
    ((3, 2), ((0, (2, 1), 0), (0, (2, 1), 1),)),
    ((1, 2), ((1, (1, 2), 0), (1, (1, 2), 1),)),
    ((2, 3), ()),
    ((1, 3), ()),
    ((3, 3), ()),
    ((0, 3), ()),
    ((1, 1), (
        (0, (1, 1), 0), (0, (3, 3), 0), (1, (1, 1), 0), (0, (1, 1), 1),
        (0, (3, 3), 1),
    )),
    ((1, 0), (
        (1, (3, 3), 0), (1, (3, 3), 1), (1, (1, 1), 1),
    )),
    ((3, 0), ()),
    ((0, 1), (
        (0, (0, 1), 0), (0, (0, 3), 0), (1, (1, 0), 0),
    )),
    ((0, 0), (
        (1, (3, 0), 0), (0, (0, 1), 1), (0, (0, 3), 1), (1, (1, 0), 1),
        (1, (3, 0), 1), (0, (0, 0), 0), (1, (0, 0), 0),
    )),
)
LAST = (
    (0, (0, 3), 0), (1, (1, 0), 0), (1, (3, 0), 0), (0, (0, 1), 0),
    (0, (0, 3), 1), (1, (1, 0), 1), (1, (3, 0), 1), (0, (0, 1), 1),
)
TABLES_AFTER = 4
ORDER = tuple(entry[0] for entry in PLAN)


def parent(route, o):
    dx, dy = STEPS[TREES[route][o]]
    return ((o[0] + dx) % SIDE, (o[1] + dy) % SIDE)


def children(route, o):
    return [v for v in TREES[route] if parent(route, v) == o]


INNER = [[v for v in tree if children(route, v)] for route, tree in enumerate(TREES)]
LEAVES = [[v for v in tree if not children(route, v)] for route, tree in enumerate(TREES)]


def coded(values):
    word = sum(v << (2 * k) for k, v in enumerate(values))
    return word - (1 << 32) if word >= 1 << 31 else word


def kernel(
    ints_in, fields_ref, weights_ref, out_ref,
    ints, cells, wts, part, col_own, col_send, col_recv, turns, early, tab_send, tab_recv, tab, sums, sums_in,
    *rest,
):
    raw_in = {}
    for route in range(ROUTES):
        for v in LEAVES[route]:
            raw_in[route, v] = rest[len(raw_in)]
    send_sem, recv_sem, field_sem, weight_sem, tab_sem, ints_sem = rest[len(raw_in):]
    bx, rows, width = fields_ref.shape
    cap, writers = ints.shape[1] // 2, ints.shape[2]
    tiles = out_ref.shape[0]
    height = rows // ROUTES
    share = tiles // PARTS
    faces = lax.axis_size("face")
    face = lax.axis_index("face")
    blk = lax.axis_index("blk")
    px, py = blk // SIDE, lax.rem(blk, SIDE)

    def at(a, b):
        return lax.rem(px + a, SIDE) * SIDE + lax.rem(py + b, SIDE)

    def writer(o):
        return at((SIDE - o[0]) % SIDE, (SIDE - o[1]) % SIDE)

    near = {name: (face, at(*step)) for name, step in STEPS.items()}
    up, down = lax.rem(face + 1, faces), lax.rem(face + faces - 1, faces)
    right, left = lax.rem(blk + 1, writers), lax.rem(blk + writers - 1, writers)
    barrier = pltpu.get_barrier_semaphore()
    greeted = [(up, blk), (down, blk), (face, left), (face, right)] + list(near.values())
    for peer in greeted:
        pl.semaphore_signal(barrier, inc=1, device_id=peer, device_id_type=MESH)

    fields_in = []
    step = bx // CHUNKS
    for i in range(CHUNKS):
        copy = pltpu.make_async_copy(
            fields_ref.at[pl.ds(i * step, step)], cells.at[pl.ds(1 + i * step, step)], field_sem.at[i]
        )
        copy.start()
        fields_in.append(copy)
    ints_copy = pltpu.make_async_copy(ints_in, ints, ints_sem)
    ints_copy.start()
    weights_in = [
        pltpu.make_async_copy(weights_ref.at[0, writer(o)], wts.at[k, :, pl.ds(0, weights_ref.shape[3])], weight_sem.at[k])
        for k, o in enumerate(ORDER)
    ]

    messages = []

    def message(src, dst, peer):
        i = len(messages)
        messages.append(
            pltpu.make_async_remote_copy(
                src_ref=src, dst_ref=dst, send_sem=send_sem.at[i], recv_sem=recv_sem.at[i],
                device_id=peer, device_id_type=MESH,
            )
        )
        return messages[i]

    halo = [
        message(fields_ref.at[bx - 1], cells.at[0], (up, blk)),
        message(fields_ref.at[0], cells.at[bx + 1], (down, blk)),
        message(col_send.at[0], col_recv.at[0], (face, right)),
        message(col_send.at[1], col_recv.at[1], (face, left)),
    ]
    tables = [message(tab_send, tab_recv.at[i], near[name]) for i, name in enumerate(STEPS)]
    raw, summed = {}, {}
    for route, tree in enumerate(TREES):
        rs = pl.ds(route * height, height)
        for v in LEAVES[route]:
            raw[route, v] = message(
                part.at[ORDER.index(v), pl.ds(0, cap), rs], raw_in[route, v].at[pl.ds(0, cap)], near[tree[v]]
            )
        for i, v in enumerate(INNER[route]):
            for h in range(PARTS):
                some = pl.ds(h * share, share)
                summed[route, v, h] = message(sums.at[route, i, some], sums_in.at[route, i, some], near[tree[v]])

    depth = weights_ref.shape[3]
    group = width // cap

    def clear(k, carry):
        for c in range(cap):
            wts[k, c, pl.ds(depth, width), :] = jnp.zeros((width, wts.shape[3]), wts.dtype)
        return carry

    lax.fori_loop(0, writers, clear, 0)

    pl.semaphore_wait(barrier, len(greeted))
    halo[0].start()
    halo[1].start()

    lanes = lax.broadcasted_iota(jnp.int32, (rows, width), 1)
    edges = (jnp.zeros((rows, width), jnp.float32), jnp.zeros((rows, width), jnp.float32))
    for i in range(CHUNKS):
        fields_in[i].wait()
        if i >= CHUNKS // 2:
            weights_in[i - CHUNKS // 2].start()

        def pick(j, edges):
            x = i * step + j
            turned = pltpu.roll(cells[1 + x], lax.rem(x + 1, width), 1)
            return (
                jnp.where(lanes == x, turned, edges[0]),
                jnp.where(lanes == lax.rem(x + 1, width), turned, edges[1]),
            )

        edges = lax.fori_loop(0, step, pick, edges, unroll=4)
    for i in range(2):
        col_own[i] = edges[i]
        col_send[i] = edges[i].astype(col_send.dtype)
    halo[2].start()
    halo[3].start()
    for copy in weights_in[CHUNKS - CHUNKS // 2:]:
        copy.start()

    ints_copy.wait()
    lane = lax.broadcasted_iota(jnp.int32, (1, 128), 1)

    def make_row(d, carry):
        row = jnp.full((1, 128), cap, jnp.int32)
        for c in range(cap):
            target = jnp.where(c < ints[0, 2 * cap, d], ints[0, cap + c, d], 127)
            row = jnp.where(lane == target, c, row)
        tab_send[pl.ds(d, 1), :] = row
        return carry

    lax.fori_loop(0, writers, make_row, 0)
    for copy in tables:
        copy.start()
    for buf in raw_in.values():
        buf[cap] = jnp.zeros((height, width), buf.dtype)
    for k, o in enumerate(ORDER):
        if o not in LEAVES[0] or o not in LEAVES[1]:
            part[k, cap] = jnp.zeros((rows, width), part.dtype)
    group_row = lax.broadcasted_iota(jnp.int32, (group, wts.shape[3]), 0)
    turn_row = lax.broadcasted_iota(jnp.int32, (2 * width, width), 0)
    code_x = jnp.int32(coded([(SIDE - o[0]) % SIDE for o in ORDER]))
    code_y = jnp.int32(coded([(SIDE - o[1]) % SIDE for o in ORDER]))

    def writer_at(k):
        return at((code_x >> (2 * k)) & 3, (code_y >> (2 * k)) & 3)

    def stack(x):
        value = cells[x + 1]
        grad_x = cells[x + 2] - cells[x]
        grad_y = pltpu.roll(value, width - 1, 1) - pltpu.roll(value, 1, 1)
        return jnp.concatenate([value + value, grad_x, grad_y], axis=1).astype(jnp.bfloat16)

    def turn(d):
        where_from = jnp.full((1, width), -1, jnp.int32)
        for c in range(cap):
            x = ints[0, c, d]
            where_from = jnp.where(lane == c * group, x, where_from)
            where_from = jnp.where(lane == c * group + group - 1, width + lax.rem(x + 1, width), where_from)
        chosen = jnp.where(turn_row == where_from, 1.0, 0.0).astype(jnp.bfloat16)
        return jnp.dot(turns[...], chosen, preferred_element_type=jnp.float32).astype(jnp.bfloat16)

    def edge_rows(k):
        for c in range(cap):
            first = wts[k, c, pl.ds(2 * width, group), :].astype(jnp.float32)
            final = wts[k, c, pl.ds(3 * width - group, group), :].astype(jnp.float32)
            edge = jnp.where(group_row == 0, first, jnp.where(group_row == group - 1, final, 0.0))
            wts[k, c, pl.ds(depth + c * group, group), :] = edge.astype(wts.dtype)

    halo[0].wait_recv()
    halo[1].wait_recv()
    weights_in[0].wait()
    edge_rows(0)
    d_first = writer(ORDER[0])

    def begin(c, carry):
        early[c] = jnp.dot(stack(ints[0, c, d_first]), wts[0, c, pl.ds(0, depth), :], preferred_element_type=jnp.float32)
        return carry

    lax.fori_loop(0, cap, begin, 0, unroll=4)
    halo[2].wait_recv()
    halo[3].wait_recv()
    turns[:, pl.ds(0, width)] = (col_own[0] - col_recv[0].astype(jnp.float32)).astype(turns.dtype)
    turns[:, pl.ds(width, width)] = (col_recv[1].astype(jnp.float32) - col_own[1]).astype(turns.dtype)
    turned = turn(d_first)
    for c in range(cap):
        product = early[c] + jnp.dot(turned, wts[0, c, pl.ds(depth, width), :], preferred_element_type=jnp.float32)
        part[0, c] = product.astype(part.dtype)
    for route in range(ROUTES):
        if ORDER[0] in LEAVES[route]:
            raw[route, ORDER[0]].start()

    def read_tables():
        for copy in tables:
            copy.wait_recv()
        sources = [tab_recv.at[i] for i in range(len(STEPS))] + [tab_send]
        copies = [pltpu.make_async_copy(src, tab.at[i], tab_sem.at[i]) for i, src in enumerate(sources)]
        for copy in copies:
            copy.start()
        for copy in copies:
            copy.wait()

    here = set()

    def gather(route, o, h, store):
        d = writer(o)
        k = ORDER.index(o)
        rs = pl.ds(route * height, height)
        below = children(route, o)
        plain = [v for v in below if v in LEAVES[route]]
        dense = [INNER[route].index(v) for v in below if v in INNER[route]]
        if o == (0, 0):
            dense = []
        for v in plain:
            if (route, v) not in here:
                raw[route, v].wait_recv()
                here.add((route, v))
        for i in dense:
            summed[route, INNER[route][i], h].wait_recv()
        ways = list(STEPS)

        def one(j, carry):
            t = h * share + j
            total = part[k, tab[len(ways), d, t], rs, :].astype(jnp.float32)
            for v in plain:
                slot = tab[ways.index(TREES[route][v]), d, t]
                total += raw_in[route, v][slot].astype(jnp.float32)
            for i in dense:
                total += sums_in[route, i, t].astype(jnp.float32)
            store(t, total)
            return carry

        lax.fori_loop(0, share, one, 0, unroll=8)

    def follow(route, o, h):
        if o == (0, 0):
            def store(t, total):
                out_ref[t, pl.ds(route * height, height), :] = total * 0.5

            for part_of in range(PARTS):
                gather(route, o, part_of, store)
        else:
            i = INNER[route].index(o)

            def store(t, total):
                sums[route, i, t] = total.astype(sums.dtype)

            gather(route, o, h, store)
            summed[route, o, h].start()

    def products(k, turned):
        d = writer_at(k)
        pltpu.make_async_copy(weights_ref.at[0, 0], wts.at[k, :, pl.ds(0, depth)], weight_sem.at[k]).wait()
        edge_rows(k)
        later = turn(writer_at(lax.rem(k + 1, len(PLAN))))
        for c in range(cap):
            stacked = jnp.concatenate([stack(ints[0, c, d]), turned], axis=1)
            product = jnp.dot(stacked, wts[k, c], preferred_element_type=jnp.float32)
            part[k, c] = product.astype(part.dtype)

        for i, (o, sums_after) in enumerate(PLAN):
            if i == 0:
                continue
            ready = [raw[route, o] for route in range(ROUTES) if o in LEAVES[route]]
            if i == len(PLAN) - 1:
                sums_after = ()
            if ready or sums_after or i == TABLES_AFTER:
                @pl.when(k == i)
                def _():
                    for copy in ready:
                        copy.start()
                    if i == TABLES_AFTER:
                        read_tables()
                    for entry in sums_after:
                        follow(*entry)
        return later

    lax.fori_loop(1, len(PLAN), products, turn(writer(ORDER[1])))
    for entry in PLAN[-1][1]:
        follow(*entry)
    for route, v, h in LAST:
        rs = pl.ds(route * height, height)
        i = INNER[route].index(v)
        summed[route, v, h].wait_recv()

        def add(j, carry):
            t = h * share + j
            out_ref[t, rs, :] += sums_in[route, i, t].astype(jnp.float32) * 0.5
            return carry

        lax.fori_loop(0, share, add, 0, unroll=8)
    for copy in messages:
        copy.wait_send()


def on_device(fields, weights, src_tile, tgt_tile, counts):
    bx, rows, width = fields.shape
    _, writers, cap, depth, tile_cells = weights.shape
    tiles = 16
    height = rows // ROUTES
    leaves = sum(len(some) for some in LEAVES)
    inner = len(INNER[0])
    messages = 8 + leaves + ROUTES * inner * PARTS
    bf16 = jnp.bfloat16
    ints = jnp.concatenate(
        [jnp.swapaxes(src_tile, 1, 2), jnp.swapaxes(tgt_tile, 1, 2), counts[:, None, :]], axis=1
    )
    return pl.pallas_call(
        kernel,
        out_shape=jax.ShapeDtypeStruct((tiles, rows, tile_cells), jnp.float32),
        in_specs=[pl.BlockSpec(memory_space=pl.ANY)] * 3,
        out_specs=pl.BlockSpec(memory_space=pltpu.VMEM),
        scratch_shapes=[
            pltpu.SMEM((1, 2 * cap + 1, writers), jnp.int32),
            pltpu.VMEM((bx + 2, rows, width), jnp.float32),
            pltpu.VMEM((writers, cap, depth + width, tile_cells), bf16),
            pltpu.VMEM((writers, cap + 1, rows, tile_cells), bf16),
            pltpu.VMEM((2, rows, width), jnp.float32),
            pltpu.VMEM((2, rows, width), bf16),
            pltpu.VMEM((2, rows, width), bf16),
            pltpu.VMEM((rows, 2 * width), bf16),
            pltpu.VMEM((cap, rows, tile_cells), jnp.float32),
            pltpu.VMEM((writers, 128), jnp.int32),
            pltpu.VMEM((len(STEPS), writers, 128), jnp.int32),
            pltpu.SMEM((len(STEPS) + 1, writers, 128), jnp.int32),
            pltpu.VMEM((ROUTES, inner, tiles, height, tile_cells), bf16),
            pltpu.VMEM((ROUTES, inner, tiles, height, tile_cells), bf16),
        ]
        + [pltpu.VMEM((cap + 1, height, tile_cells), bf16)] * leaves
        + [
            pltpu.SemaphoreType.DMA((messages,)),
            pltpu.SemaphoreType.DMA((messages,)),
            pltpu.SemaphoreType.DMA((CHUNKS,)),
            pltpu.SemaphoreType.DMA((writers,)),
            pltpu.SemaphoreType.DMA((len(STEPS) + 1,)),
            pltpu.SemaphoreType.DMA,
        ],
        compiler_params=pltpu.CompilerParams(
            collective_id=0, has_side_effects=True, vmem_limit_bytes=52 * 1024 * 1024
        ),
        cost_estimate=pl.CostEstimate(flops=1208000000, bytes_accessed=19700000, transcendentals=0),
    )(ints, fields, weights)


def solution(mesh):
    placed = (
        P("face", None, "blk"),
        P(("face", "blk"), None, None, None, None),
        P(("face", "blk"), None, None),
        P(("face", "blk"), None, None),
        P(("face", "blk"), None),
    )
    return jax.shard_map(
        on_device,
        mesh=mesh,
        in_specs=placed,
        out_specs=P(("face", "blk"), None, None),
        check_vma=False,
    )
```

```python
import jax
import jax.numpy as jnp
from jax import lax
from jax.experimental import pallas as pl
from jax.experimental.pallas import tpu as pltpu
from jax.sharding import PartitionSpec as P

MESH = pl.DeviceIdType.MESH
SIDE = 4
CHUNKS = 8
ROUTES = 2
PARTS = 2
STEPS = {"x+": (1, 0), "x-": (3, 0), "y+": (0, 1), "y-": (0, 3)}
TREES = (
    {
        (0, 1): "y-", (0, 2): "y+", (0, 3): "y+", (1, 0): "x-", (1, 1): "x-",
        (1, 2): "y-", (1, 3): "x-", (2, 0): "y+", (2, 1): "x-", (2, 2): "y-",
        (2, 3): "x+", (3, 0): "x+", (3, 1): "x+", (3, 2): "y+", (3, 3): "x+",
    },
    {
        (0, 1): "y-", (0, 2): "x+", (0, 3): "y+", (1, 0): "x-", (1, 1): "y-",
        (1, 2): "y-", (1, 3): "y+", (2, 0): "x+", (2, 1): "x-", (2, 2): "x-",
        (2, 3): "x+", (3, 0): "x+", (3, 1): "y-", (3, 2): "y+", (3, 3): "y+",
    },
)
PLAN = (
    ((2, 0), ()),
    ((2, 2), ()),
    ((0, 2), ()),
    ((2, 1), ()),
    ((3, 1), ()),
    ((3, 2), ((0, (2, 1), 0), (0, (2, 1), 1),)),
    ((1, 2), ((1, (1, 2), 0), (1, (1, 2), 1),)),
    ((2, 3), ()),
    ((1, 3), ()),
    ((3, 3), ()),
    ((0, 3), ()),
    ((1, 1), (
        (0, (1, 1), 0), (0, (3, 3), 0), (1, (1, 1), 0), (0, (1, 1), 1),
        (0, (3, 3), 1),
    )),
    ((1, 0), (
        (1, (3, 3), 0), (1, (3, 3), 1), (1, (1, 1), 1),
    )),
    ((3, 0), ()),
    ((0, 1), (
        (0, (0, 1), 0), (0, (0, 3), 0), (1, (1, 0), 0),
    )),
    ((0, 0), (
        (1, (3, 0), 0), (0, (0, 1), 1), (0, (0, 3), 1), (1, (1, 0), 1),
        (1, (3, 0), 1), (0, (0, 0), 0), (1, (0, 0), 0),
    )),
)
LAST = (
    (0, (0, 3), 0), (1, (1, 0), 0), (1, (3, 0), 0), (0, (0, 1), 0),
    (0, (0, 3), 1), (1, (1, 0), 1), (1, (3, 0), 1), (0, (0, 1), 1),
)
TABLES_AFTER = 4
ORDER = tuple(entry[0] for entry in PLAN)


def parent(route, o):
    dx, dy = STEPS[TREES[route][o]]
    return ((o[0] + dx) % SIDE, (o[1] + dy) % SIDE)


def children(route, o):
    return [v for v in TREES[route] if parent(route, v) == o]


INNER = [[v for v in tree if children(route, v)] for route, tree in enumerate(TREES)]
LEAVES = [[v for v in tree if not children(route, v)] for route, tree in enumerate(TREES)]


def coded(values):
    word = sum(v << (2 * k) for k, v in enumerate(values))
    return word - (1 << 32) if word >= 1 << 31 else word


def kernel(
    ints_in, fields_ref, weights_ref, out_ref,
    ints, cells, wts, part, col_own, col_send, col_recv, turns, early, tab_send, tab_recv, tab, sums, sums_in,
    *rest,
):
    raw_in = {}
    for route in range(ROUTES):
        for v in LEAVES[route]:
            raw_in[route, v] = rest[len(raw_in)]
    send_sem, recv_sem, field_sem, weight_sem, tab_sem, ints_sem = rest[len(raw_in):]
    bx, rows, width = fields_ref.shape
    cap, writers = ints.shape[1] // 2, ints.shape[2]
    tiles = out_ref.shape[0]
    height = rows // ROUTES
    share = tiles // PARTS
    faces = lax.axis_size("face")
    face = lax.axis_index("face")
    blk = lax.axis_index("blk")
    px, py = blk // SIDE, lax.rem(blk, SIDE)

    def at(a, b):
        return lax.rem(px + a, SIDE) * SIDE + lax.rem(py + b, SIDE)

    def writer(o):
        return at((SIDE - o[0]) % SIDE, (SIDE - o[1]) % SIDE)

    near = {name: (face, at(*step)) for name, step in STEPS.items()}
    up, down = lax.rem(face + 1, faces), lax.rem(face + faces - 1, faces)
    right, left = lax.rem(blk + 1, writers), lax.rem(blk + writers - 1, writers)
    barrier = pltpu.get_barrier_semaphore()
    greeted = [(up, blk), (down, blk), (face, left), (face, right)] + list(near.values())
    for peer in greeted:
        pl.semaphore_signal(barrier, inc=1, device_id=peer, device_id_type=MESH)

    fields_in = []
    step = bx // CHUNKS
    for i in range(CHUNKS):
        copy = pltpu.make_async_copy(
            fields_ref.at[pl.ds(i * step, step)], cells.at[pl.ds(1 + i * step, step)], field_sem.at[i]
        )
        copy.start()
        fields_in.append(copy)
    ints_copy = pltpu.make_async_copy(ints_in, ints, ints_sem)
    ints_copy.start()
    weights_in = [
        pltpu.make_async_copy(weights_ref.at[0, writer(o)], wts.at[k, :, pl.ds(0, weights_ref.shape[3])], weight_sem.at[k])
        for k, o in enumerate(ORDER)
    ]

    messages = []

    def message(src, dst, peer):
        i = len(messages)
        messages.append(
            pltpu.make_async_remote_copy(
                src_ref=src, dst_ref=dst, send_sem=send_sem.at[i], recv_sem=recv_sem.at[i],
                device_id=peer, device_id_type=MESH,
            )
        )
        return messages[i]

    halo = [
        message(fields_ref.at[bx - 1], cells.at[0], (up, blk)),
        message(fields_ref.at[0], cells.at[bx + 1], (down, blk)),
        message(col_send.at[0], col_recv.at[0], (face, right)),
        message(col_send.at[1], col_recv.at[1], (face, left)),
    ]
    tables = [message(tab_send, tab_recv.at[i], near[name]) for i, name in enumerate(STEPS)]
    raw, summed = {}, {}
    for route, tree in enumerate(TREES):
        rs = pl.ds(route * height, height)
        for v in LEAVES[route]:
            raw[route, v] = message(
                part.at[ORDER.index(v), pl.ds(0, cap), rs], raw_in[route, v].at[pl.ds(0, cap)], near[tree[v]]
            )
        for i, v in enumerate(INNER[route]):
            for h in range(PARTS):
                some = pl.ds(h * share, share)
                summed[route, v, h] = message(sums.at[route, i, some], sums_in.at[route, i, some], near[tree[v]])

    depth = weights_ref.shape[3]
    group = width // cap

    def clear(k, carry):
        for c in range(cap):
            wts[k, c, pl.ds(depth, width), :] = jnp.zeros((width, wts.shape[3]), wts.dtype)
        return carry

    lax.fori_loop(0, writers, clear, 0)

    pl.semaphore_wait(barrier, len(greeted))
    halo[0].start()
    halo[1].start()

    lanes = lax.broadcasted_iota(jnp.int32, (rows, width), 1)
    edges = (jnp.zeros((rows, width), jnp.float32), jnp.zeros((rows, width), jnp.float32))
    for i in range(CHUNKS):
        fields_in[i].wait()
        if i >= CHUNKS // 2:
            weights_in[i - CHUNKS // 2].start()

        def pick(j, edges):
            x = i * step + j
            turned = pltpu.roll(cells[1 + x], lax.rem(x + 1, width), 1)
            return (
                jnp.where(lanes == x, turned, edges[0]),
                jnp.where(lanes == lax.rem(x + 1, width), turned, edges[1]),
            )

        edges = lax.fori_loop(0, step, pick, edges, unroll=4)
    for i in range(2):
        col_own[i] = edges[i]
        col_send[i] = edges[i].astype(col_send.dtype)
    halo[2].start()
    halo[3].start()
    for copy in weights_in[CHUNKS - CHUNKS // 2:]:
        copy.start()

    ints_copy.wait()
    lane = lax.broadcasted_iota(jnp.int32, (1, 128), 1)

    def make_row(d, carry):
        row = jnp.full((1, 128), cap, jnp.int32)
        for c in range(cap):
            target = jnp.where(c < ints[0, 2 * cap, d], ints[0, cap + c, d], 127)
            row = jnp.where(lane == target, c, row)
        tab_send[pl.ds(d, 1), :] = row
        return carry

    lax.fori_loop(0, writers, make_row, 0)
    for copy in tables:
        copy.start()
    for buf in raw_in.values():
        buf[cap] = jnp.zeros((height, width), buf.dtype)
    for k, o in enumerate(ORDER):
        if o not in LEAVES[0] or o not in LEAVES[1]:
            part[k, cap] = jnp.zeros((rows, width), part.dtype)
    group_row = lax.broadcasted_iota(jnp.int32, (group, wts.shape[3]), 0)
    turn_row = lax.broadcasted_iota(jnp.int32, (2 * width, width), 0)
    code_x = jnp.int32(coded([(SIDE - o[0]) % SIDE for o in ORDER]))
    code_y = jnp.int32(coded([(SIDE - o[1]) % SIDE for o in ORDER]))

    def writer_at(k):
        return at((code_x >> (2 * k)) & 3, (code_y >> (2 * k)) & 3)

    def stack(x):
        value = cells[x + 1]
        grad_x = cells[x + 2] - cells[x]
        grad_y = pltpu.roll(value, width - 1, 1) - pltpu.roll(value, 1, 1)
        return jnp.concatenate([value + value, grad_x, grad_y], axis=1).astype(jnp.bfloat16)

    def turn(d):
        where_from = jnp.full((1, width), -1, jnp.int32)
        for c in range(cap):
            x = ints[0, c, d]
            where_from = jnp.where(lane == c * group, x, where_from)
            where_from = jnp.where(lane == c * group + group - 1, width + lax.rem(x + 1, width), where_from)
        chosen = jnp.where(turn_row == where_from, 1.0, 0.0).astype(jnp.bfloat16)
        return jnp.dot(turns[...], chosen, preferred_element_type=jnp.float32).astype(jnp.bfloat16)

    def edge_rows(k):
        for c in range(cap):
            first = wts[k, c, pl.ds(2 * width, group), :].astype(jnp.float32)
            final = wts[k, c, pl.ds(3 * width - group, group), :].astype(jnp.float32)
            edge = jnp.where(group_row == 0, first, jnp.where(group_row == group - 1, final, 0.0))
            wts[k, c, pl.ds(depth + c * group, group), :] = edge.astype(wts.dtype)

    halo[0].wait_recv()
    halo[1].wait_recv()
    weights_in[0].wait()
    edge_rows(0)
    d_first = writer(ORDER[0])

    def begin(c, carry):
        early[c] = jnp.dot(stack(ints[0, c, d_first]), wts[0, c, pl.ds(0, depth), :], preferred_element_type=jnp.float32)
        return carry

    lax.fori_loop(0, cap, begin, 0, unroll=4)
    halo[2].wait_recv()
    halo[3].wait_recv()
    turns[:, pl.ds(0, width)] = (col_own[0] - col_recv[0].astype(jnp.float32)).astype(turns.dtype)
    turns[:, pl.ds(width, width)] = (col_recv[1].astype(jnp.float32) - col_own[1]).astype(turns.dtype)
    turned = turn(d_first)
    for c in range(cap):
        product = early[c] + jnp.dot(turned, wts[0, c, pl.ds(depth, width), :], preferred_element_type=jnp.float32)
        part[0, c] = product.astype(part.dtype)
    for route in range(ROUTES):
        if ORDER[0] in LEAVES[route]:
            raw[route, ORDER[0]].start()

    def read_tables():
        for copy in tables:
            copy.wait_recv()
        sources = [tab_recv.at[i] for i in range(len(STEPS))] + [tab_send]
        copies = [pltpu.make_async_copy(src, tab.at[i], tab_sem.at[i]) for i, src in enumerate(sources)]
        for copy in copies:
            copy.start()
        for copy in copies:
            copy.wait()

    here = set()

    def gather(route, o, h, store):
        d = writer(o)
        k = ORDER.index(o)
        rs = pl.ds(route * height, height)
        below = children(route, o)
        plain = [v for v in below if v in LEAVES[route]]
        dense = [INNER[route].index(v) for v in below if v in INNER[route]]
        if o == (0, 0):
            dense = []
        for v in plain:
            if (route, v) not in here:
                raw[route, v].wait_recv()
                here.add((route, v))
        for i in dense:
            summed[route, INNER[route][i], h].wait_recv()
        ways = list(STEPS)

        def one(j, carry):
            t = h * share + j
            total = part[k, tab[len(ways), d, t], rs, :].astype(jnp.float32)
            for v in plain:
                slot = tab[ways.index(TREES[route][v]), d, t]
                total += raw_in[route, v][slot].astype(jnp.float32)
            for i in dense:
                total += sums_in[route, i, t].astype(jnp.float32)
            store(t, total)
            return carry

        lax.fori_loop(0, share, one, 0, unroll=8)

    def follow(route, o, h):
        if o == (0, 0):
            def store(t, total):
                out_ref[t, pl.ds(route * height, height), :] = total * 0.5

            for part_of in range(PARTS):
                gather(route, o, part_of, store)
        else:
            i = INNER[route].index(o)

            def store(t, total):
                sums[route, i, t] = total.astype(sums.dtype)

            gather(route, o, h, store)
            summed[route, o, h].start()

    def products(k, turned):
        d = writer_at(k)
        pltpu.make_async_copy(weights_ref.at[0, 0], wts.at[k, :, pl.ds(0, depth)], weight_sem.at[k]).wait()
        edge_rows(k)
        later = turn(writer_at(lax.rem(k + 1, len(PLAN))))
        for c in range(0, cap, 2):
            pair = [jnp.concatenate([stack(ints[0, c + i, d]), turned], axis=1) for i in range(2)]
            both = jnp.dot(
                jnp.concatenate(pair, axis=0),
                jnp.concatenate([wts[k, c], wts[k, c + 1]], axis=1),
                preferred_element_type=jnp.float32,
            )
            part[k, c] = both[:rows, :width].astype(part.dtype)
            part[k, c + 1] = both[rows:, width:].astype(part.dtype)

        for i, (o, sums_after) in enumerate(PLAN):
            if i == 0:
                continue
            ready = [raw[route, o] for route in range(ROUTES) if o in LEAVES[route]]
            if i == len(PLAN) - 1:
                sums_after = ()
            if ready or sums_after or i == TABLES_AFTER:
                @pl.when(k == i)
                def _():
                    for copy in ready:
                        copy.start()
                    if i == TABLES_AFTER:
                        read_tables()
                    for entry in sums_after:
                        follow(*entry)
        return later

    lax.fori_loop(1, len(PLAN), products, turn(writer(ORDER[1])))
    for entry in PLAN[-1][1]:
        follow(*entry)
    for route, v, h in LAST:
        rs = pl.ds(route * height, height)
        i = INNER[route].index(v)
        summed[route, v, h].wait_recv()

        def add(j, carry):
            t = h * share + j
            out_ref[t, rs, :] += sums_in[route, i, t].astype(jnp.float32) * 0.5
            return carry

        lax.fori_loop(0, share, add, 0, unroll=8)
    for copy in messages:
        copy.wait_send()


def on_device(fields, weights, src_tile, tgt_tile, counts):
    bx, rows, width = fields.shape
    _, writers, cap, depth, tile_cells = weights.shape
    tiles = 16
    height = rows // ROUTES
    leaves = sum(len(some) for some in LEAVES)
    inner = len(INNER[0])
    messages = 8 + leaves + ROUTES * inner * PARTS
    bf16 = jnp.bfloat16
    ints = jnp.concatenate(
        [jnp.swapaxes(src_tile, 1, 2), jnp.swapaxes(tgt_tile, 1, 2), counts[:, None, :]], axis=1
    )
    return pl.pallas_call(
        kernel,
        out_shape=jax.ShapeDtypeStruct((tiles, rows, tile_cells), jnp.float32),
        in_specs=[pl.BlockSpec(memory_space=pl.ANY)] * 3,
        out_specs=pl.BlockSpec(memory_space=pltpu.VMEM),
        scratch_shapes=[
            pltpu.SMEM((1, 2 * cap + 1, writers), jnp.int32),
            pltpu.VMEM((bx + 2, rows, width), jnp.float32),
            pltpu.VMEM((writers, cap, depth + width, tile_cells), bf16),
            pltpu.VMEM((writers, cap + 1, rows, tile_cells), bf16),
            pltpu.VMEM((2, rows, width), jnp.float32),
            pltpu.VMEM((2, rows, width), bf16),
            pltpu.VMEM((2, rows, width), bf16),
            pltpu.VMEM((rows, 2 * width), bf16),
            pltpu.VMEM((cap, rows, tile_cells), jnp.float32),
            pltpu.VMEM((writers, 128), jnp.int32),
            pltpu.VMEM((len(STEPS), writers, 128), jnp.int32),
            pltpu.SMEM((len(STEPS) + 1, writers, 128), jnp.int32),
            pltpu.VMEM((ROUTES, inner, tiles, height, tile_cells), bf16),
            pltpu.VMEM((ROUTES, inner, tiles, height, tile_cells), bf16),
        ]
        + [pltpu.VMEM((cap + 1, height, tile_cells), bf16)] * leaves
        + [
            pltpu.SemaphoreType.DMA((messages,)),
            pltpu.SemaphoreType.DMA((messages,)),
            pltpu.SemaphoreType.DMA((CHUNKS,)),
            pltpu.SemaphoreType.DMA((writers,)),
            pltpu.SemaphoreType.DMA((len(STEPS) + 1,)),
            pltpu.SemaphoreType.DMA,
        ],
        compiler_params=pltpu.CompilerParams(
            collective_id=0, has_side_effects=True, vmem_limit_bytes=52 * 1024 * 1024
        ),
        cost_estimate=pl.CostEstimate(flops=1208000000, bytes_accessed=19700000, transcendentals=0),
    )(ints, fields, weights)


def solution(mesh):
    placed = (
        P("face", None, "blk"),
        P(("face", "blk"), None, None, None, None),
        P(("face", "blk"), None, None),
        P(("face", "blk"), None, None),
        P(("face", "blk"), None),
    )
    return jax.shard_map(
        on_device,
        mesh=mesh,
        in_specs=placed,
        out_specs=P(("face", "blk"), None, None),
        check_vma=False,
    )
```

```python
import jax
import jax.numpy as jnp
from jax import lax
from jax.experimental import pallas as pl
from jax.experimental.pallas import tpu as pltpu
from jax.sharding import PartitionSpec as P

MESH = pl.DeviceIdType.MESH
SIDE = 4
CHUNKS = 8
ROUTES = 2
PARTS = 4
STEPS = {"x+": (1, 0), "x-": (3, 0), "y+": (0, 1), "y-": (0, 3)}
TREES = (
    {
        (0, 1): "x+", (0, 2): "y+", (0, 3): "y+", (1, 0): "x-", (1, 1): "y-",
        (1, 2): "y-", (1, 3): "y+", (2, 0): "x-", (2, 1): "x-", (2, 2): "x+",
        (2, 3): "x+", (3, 0): "x+", (3, 1): "y+", (3, 2): "y+", (3, 3): "x+",
    },
    {
        (0, 1): "y-", (0, 2): "y-", (0, 3): "x-", (1, 0): "x-", (1, 1): "x-",
        (1, 2): "y-", (1, 3): "y-", (2, 0): "x+", (2, 1): "x-", (2, 2): "x-",
        (2, 3): "x+", (3, 0): "x+", (3, 1): "y-", (3, 2): "y+", (3, 3): "y+",
    },
)
PLAN = (
    ((3, 1), ()),
    ((2, 2), ()),
    ((2, 1), ()),
    ((1, 3), ()),
    ((0, 1), ()),
    ((2, 3), ()),
    ((0, 2), ()),
    ((0, 3), ()),
    ((1, 2), ()),
    ((3, 2), (
        (0, (3, 2), 0), (0, (3, 2), 1), (0, (3, 2), 2), (1, (1, 2), 0),
        (1, (1, 2), 1), (1, (1, 2), 2), (0, (3, 2), 3), (1, (1, 2), 3),
    )),
    ((2, 0), ()),
    ((1, 1), ()),
    ((1, 0), ()),
    ((3, 0), ()),
    ((3, 3), ()),
    ((0, 0), (
        (0, (1, 1), 0), (1, (3, 3), 0), (0, (1, 1), 1), (1, (3, 3), 1),
        (0, (1, 1), 2), (1, (3, 3), 2), (1, (1, 1), 0), (0, (1, 1), 3),
        (0, (3, 3), 0), (1, (3, 3), 3), (1, (1, 1), 1), (0, (3, 3), 1),
        (1, (1, 1), 2), (0, (3, 3), 2), (1, (1, 1), 3), (0, (3, 3), 3),
        (1, (0, 0), 0), (0, (0, 0), 0), (0, (1, 0), 0), (1, (3, 0), 0),
        (1, (0, 1), 0), (0, (0, 3), 0), (0, (1, 0), 1), (1, (3, 0), 1),
        (1, (0, 1), 1), (0, (0, 3), 1), (0, (1, 0), 2), (1, (3, 0), 2),
        (1, (0, 1), 2), (0, (0, 3), 2), (0, (1, 0), 3), (1, (3, 0), 3),
        (1, (0, 1), 3), (0, (0, 3), 3),
    )),
)
LAST = (
    (1, (0, 1), 0), (0, (0, 3), 0), (0, (1, 0), 0), (1, (3, 0), 0),
    (1, (0, 1), 1), (0, (0, 3), 1), (0, (1, 0), 1), (1, (3, 0), 1),
    (1, (0, 1), 2), (0, (0, 3), 2), (0, (1, 0), 2), (1, (3, 0), 2),
    (1, (0, 1), 3), (0, (0, 3), 3), (0, (1, 0), 3), (1, (3, 0), 3),
)
TABLES_AFTER = 8
ORDER = tuple(entry[0] for entry in PLAN)


def parent(route, o):
    dx, dy = STEPS[TREES[route][o]]
    return ((o[0] + dx) % SIDE, (o[1] + dy) % SIDE)


def children(route, o):
    return [v for v in TREES[route] if parent(route, v) == o]


INNER = [[v for v in tree if children(route, v)] for route, tree in enumerate(TREES)]
LEAVES = [[v for v in tree if not children(route, v)] for route, tree in enumerate(TREES)]


def coded(values):
    word = sum(v << (2 * k) for k, v in enumerate(values))
    return word - (1 << 32) if word >= 1 << 31 else word


def kernel(
    ints_in, fields_ref, weights_ref, out_ref,
    ints, cells, wts, part, col_own, col_send, col_recv, turns, early, tab_send, tab_recv, tab, sums, sums_in,
    *rest,
):
    raw_in = {}
    for route in range(ROUTES):
        for v in LEAVES[route]:
            raw_in[route, v] = rest[len(raw_in)]
    send_sem, recv_sem, field_sem, weight_sem, tab_sem, ints_sem = rest[len(raw_in):]
    bx, rows, width = fields_ref.shape
    cap, writers = ints.shape[1] // 2, ints.shape[2]
    tiles = out_ref.shape[0]
    height = rows // ROUTES
    share = tiles // PARTS
    faces = lax.axis_size("face")
    face = lax.axis_index("face")
    blk = lax.axis_index("blk")
    px, py = blk // SIDE, lax.rem(blk, SIDE)

    def at(a, b):
        return lax.rem(px + a, SIDE) * SIDE + lax.rem(py + b, SIDE)

    def writer(o):
        return at((SIDE - o[0]) % SIDE, (SIDE - o[1]) % SIDE)

    near = {name: (face, at(*step)) for name, step in STEPS.items()}
    up, down = lax.rem(face + 1, faces), lax.rem(face + faces - 1, faces)
    right, left = lax.rem(blk + 1, writers), lax.rem(blk + writers - 1, writers)
    barrier = pltpu.get_barrier_semaphore()
    greeted = [(up, blk), (down, blk), (face, left), (face, right)] + list(near.values())
    for peer in greeted:
        pl.semaphore_signal(barrier, inc=1, device_id=peer, device_id_type=MESH)

    fields_in = []
    step = bx // CHUNKS
    for i in range(CHUNKS):
        copy = pltpu.make_async_copy(
            fields_ref.at[pl.ds(i * step, step)], cells.at[pl.ds(1 + i * step, step)], field_sem.at[i]
        )
        copy.start()
        fields_in.append(copy)
    ints_copy = pltpu.make_async_copy(ints_in, ints, ints_sem)
    ints_copy.start()
    weights_in = [
        pltpu.make_async_copy(weights_ref.at[0, writer(o)], wts.at[k, :, pl.ds(0, weights_ref.shape[3])], weight_sem.at[k])
        for k, o in enumerate(ORDER)
    ]

    messages = []

    def message(src, dst, peer):
        i = len(messages)
        messages.append(
            pltpu.make_async_remote_copy(
                src_ref=src, dst_ref=dst, send_sem=send_sem.at[i], recv_sem=recv_sem.at[i],
                device_id=peer, device_id_type=MESH,
            )
        )
        return messages[i]

    halo = [
        message(fields_ref.at[bx - 1], cells.at[0], (up, blk)),
        message(fields_ref.at[0], cells.at[bx + 1], (down, blk)),
        message(col_send.at[0], col_recv.at[0], (face, right)),
        message(col_send.at[1], col_recv.at[1], (face, left)),
    ]
    tables = [message(tab_send, tab_recv.at[i], near[name]) for i, name in enumerate(STEPS)]
    raw, summed = {}, {}
    for route, tree in enumerate(TREES):
        rs = pl.ds(route * height, height)
        for v in LEAVES[route]:
            raw[route, v] = message(
                part.at[ORDER.index(v), pl.ds(0, cap), rs], raw_in[route, v].at[pl.ds(0, cap)], near[tree[v]]
            )
        for i, v in enumerate(INNER[route]):
            for h in range(PARTS):
                some = pl.ds(h * share, share)
                summed[route, v, h] = message(sums.at[route, i, some], sums_in.at[route, i, some], near[tree[v]])

    depth = weights_ref.shape[3]
    group = width // cap

    def clear(k, carry):
        for c in range(cap):
            wts[k, c, pl.ds(depth, width), :] = jnp.zeros((width, wts.shape[3]), wts.dtype)
        return carry

    lax.fori_loop(0, writers, clear, 0)

    pl.semaphore_wait(barrier, len(greeted))
    halo[0].start()
    halo[1].start()

    lanes = lax.broadcasted_iota(jnp.int32, (rows, width), 1)
    edges = (jnp.zeros((rows, width), jnp.float32), jnp.zeros((rows, width), jnp.float32))
    for i in range(CHUNKS):
        fields_in[i].wait()
        if i >= CHUNKS // 2:
            weights_in[i - CHUNKS // 2].start()

        def pick(j, edges):
            x = i * step + j
            turned = pltpu.roll(cells[1 + x], lax.rem(x + 1, width), 1)
            return (
                jnp.where(lanes == x, turned, edges[0]),
                jnp.where(lanes == lax.rem(x + 1, width), turned, edges[1]),
            )

        edges = lax.fori_loop(0, step, pick, edges, unroll=4)
    for i in range(2):
        col_own[i] = edges[i]
        col_send[i] = edges[i].astype(col_send.dtype)
    halo[2].start()
    halo[3].start()
    for copy in weights_in[CHUNKS - CHUNKS // 2:]:
        copy.start()

    ints_copy.wait()
    lane = lax.broadcasted_iota(jnp.int32, (1, 128), 1)

    def make_row(d, carry):
        row = jnp.full((1, 128), cap, jnp.int32)
        for c in range(cap):
            target = jnp.where(c < ints[0, 2 * cap, d], ints[0, cap + c, d], 127)
            row = jnp.where(lane == target, c, row)
        tab_send[pl.ds(d, 1), :] = row
        return carry

    lax.fori_loop(0, writers, make_row, 0)
    for copy in tables:
        copy.start()
    for buf in raw_in.values():
        buf[cap] = jnp.zeros((height, width), buf.dtype)
    for k, o in enumerate(ORDER):
        if o not in LEAVES[0] or o not in LEAVES[1]:
            part[k, cap] = jnp.zeros((rows, width), part.dtype)
    group_row = lax.broadcasted_iota(jnp.int32, (group, wts.shape[3]), 0)
    turn_row = lax.broadcasted_iota(jnp.int32, (2 * width, width), 0)
    code_x = jnp.int32(coded([(SIDE - o[0]) % SIDE for o in ORDER]))
    code_y = jnp.int32(coded([(SIDE - o[1]) % SIDE for o in ORDER]))

    def writer_at(k):
        return at((code_x >> (2 * k)) & 3, (code_y >> (2 * k)) & 3)

    def stack(x):
        value = cells[x + 1]
        grad_x = cells[x + 2] - cells[x]
        grad_y = pltpu.roll(value, width - 1, 1) - pltpu.roll(value, 1, 1)
        return jnp.concatenate([value + value, grad_x, grad_y], axis=1).astype(jnp.bfloat16)

    def turn(d):
        where_from = jnp.full((1, width), -1, jnp.int32)
        for c in range(cap):
            x = ints[0, c, d]
            where_from = jnp.where(lane == c * group, x, where_from)
            where_from = jnp.where(lane == c * group + group - 1, width + lax.rem(x + 1, width), where_from)
        chosen = jnp.where(turn_row == where_from, 1.0, 0.0).astype(jnp.bfloat16)
        return jnp.dot(turns[...], chosen, preferred_element_type=jnp.float32).astype(jnp.bfloat16)

    def edge_rows(k):
        for c in range(cap):
            first = wts[k, c, pl.ds(2 * width, group), :].astype(jnp.float32)
            final = wts[k, c, pl.ds(3 * width - group, group), :].astype(jnp.float32)
            edge = jnp.where(group_row == 0, first, jnp.where(group_row == group - 1, final, 0.0))
            wts[k, c, pl.ds(depth + c * group, group), :] = edge.astype(wts.dtype)

    halo[0].wait_recv()
    halo[1].wait_recv()
    weights_in[0].wait()
    edge_rows(0)
    d_first = writer(ORDER[0])

    def begin(c, carry):
        early[c] = jnp.dot(stack(ints[0, c, d_first]), wts[0, c, pl.ds(0, depth), :], preferred_element_type=jnp.float32)
        return carry

    lax.fori_loop(0, cap, begin, 0, unroll=4)
    halo[2].wait_recv()
    halo[3].wait_recv()
    turns[:, pl.ds(0, width)] = (col_own[0] - col_recv[0].astype(jnp.float32)).astype(turns.dtype)
    turns[:, pl.ds(width, width)] = (col_recv[1].astype(jnp.float32) - col_own[1]).astype(turns.dtype)
    turned = turn(d_first)
    for c in range(cap):
        product = early[c] + jnp.dot(turned, wts[0, c, pl.ds(depth, width), :], preferred_element_type=jnp.float32)
        part[0, c] = product.astype(part.dtype)
    for route in range(ROUTES):
        if ORDER[0] in LEAVES[route]:
            raw[route, ORDER[0]].start()

    def read_tables():
        for copy in tables:
            copy.wait_recv()
        sources = [tab_recv.at[i] for i in range(len(STEPS))] + [tab_send]
        copies = [pltpu.make_async_copy(src, tab.at[i], tab_sem.at[i]) for i, src in enumerate(sources)]
        for copy in copies:
            copy.start()
        for copy in copies:
            copy.wait()

    here = set()

    def gather(route, o, h, store):
        d = writer(o)
        k = ORDER.index(o)
        rs = pl.ds(route * height, height)
        below = children(route, o)
        plain = [v for v in below if v in LEAVES[route]]
        dense = [INNER[route].index(v) for v in below if v in INNER[route]]
        if o == (0, 0):
            dense = []
        for v in plain:
            if (route, v) not in here:
                raw[route, v].wait_recv()
                here.add((route, v))
        for i in dense:
            summed[route, INNER[route][i], h].wait_recv()
        ways = list(STEPS)

        def one(j, carry):
            t = h * share + j
            total = part[k, tab[len(ways), d, t], rs, :].astype(jnp.float32)
            for v in plain:
                slot = tab[ways.index(TREES[route][v]), d, t]
                total += raw_in[route, v][slot].astype(jnp.float32)
            for i in dense:
                total += sums_in[route, i, t].astype(jnp.float32)
            store(t, total)
            return carry

        lax.fori_loop(0, share, one, 0, unroll=4)

    def follow(route, o, h):
        if o == (0, 0):
            def store(t, total):
                out_ref[t, pl.ds(route * height, height), :] = total * 0.5

            for part_of in range(PARTS):
                gather(route, o, part_of, store)
        else:
            i = INNER[route].index(o)

            def store(t, total):
                sums[route, i, t] = total.astype(sums.dtype)

            gather(route, o, h, store)
            summed[route, o, h].start()

    def products(k, turned):
        d = writer_at(k)
        pltpu.make_async_copy(weights_ref.at[0, 0], wts.at[k, :, pl.ds(0, depth)], weight_sem.at[k]).wait()
        edge_rows(k)
        later = turn(writer_at(lax.rem(k + 1, len(PLAN))))
        for c in range(cap):
            stacked = jnp.concatenate([stack(ints[0, c, d]), turned], axis=1)
            product = jnp.dot(stacked, wts[k, c], preferred_element_type=jnp.float32)
            part[k, c] = product.astype(part.dtype)

        for i, (o, sums_after) in enumerate(PLAN):
            if i == 0:
                continue
            ready = [raw[route, o] for route in range(ROUTES) if o in LEAVES[route]]
            if i == len(PLAN) - 1:
                sums_after = ()
            if ready or sums_after or i == TABLES_AFTER:
                @pl.when(k == i)
                def _():
                    for copy in ready:
                        copy.start()
                    if i == TABLES_AFTER:
                        read_tables()
                    for entry in sums_after:
                        follow(*entry)
        return later

    lax.fori_loop(1, len(PLAN), products, turn(writer(ORDER[1])))
    for entry in PLAN[-1][1]:
        follow(*entry)
    for route, v, h in LAST:
        rs = pl.ds(route * height, height)
        i = INNER[route].index(v)
        summed[route, v, h].wait_recv()

        def add(j, carry):
            t = h * share + j
            out_ref[t, rs, :] += sums_in[route, i, t].astype(jnp.float32) * 0.5
            return carry

        lax.fori_loop(0, share, add, 0, unroll=4)
    for copy in messages:
        copy.wait_send()


def on_device(fields, weights, src_tile, tgt_tile, counts):
    bx, rows, width = fields.shape
    _, writers, cap, depth, tile_cells = weights.shape
    tiles = 16
    height = rows // ROUTES
    leaves = sum(len(some) for some in LEAVES)
    inner = len(INNER[0])
    messages = 8 + leaves + ROUTES * inner * PARTS
    bf16 = jnp.bfloat16
    ints = jnp.concatenate(
        [jnp.swapaxes(src_tile, 1, 2), jnp.swapaxes(tgt_tile, 1, 2), counts[:, None, :]], axis=1
    )
    return pl.pallas_call(
        kernel,
        out_shape=jax.ShapeDtypeStruct((tiles, rows, tile_cells), jnp.float32),
        in_specs=[pl.BlockSpec(memory_space=pl.ANY)] * 3,
        out_specs=pl.BlockSpec(memory_space=pltpu.VMEM),
        scratch_shapes=[
            pltpu.SMEM((1, 2 * cap + 1, writers), jnp.int32),
            pltpu.VMEM((bx + 2, rows, width), jnp.float32),
            pltpu.VMEM((writers, cap, depth + width, tile_cells), bf16),
            pltpu.VMEM((writers, cap + 1, rows, tile_cells), bf16),
            pltpu.VMEM((2, rows, width), jnp.float32),
            pltpu.VMEM((2, rows, width), bf16),
            pltpu.VMEM((2, rows, width), bf16),
            pltpu.VMEM((rows, 2 * width), bf16),
            pltpu.VMEM((cap, rows, tile_cells), jnp.float32),
            pltpu.VMEM((writers, 128), jnp.int32),
            pltpu.VMEM((len(STEPS), writers, 128), jnp.int32),
            pltpu.SMEM((len(STEPS) + 1, writers, 128), jnp.int32),
            pltpu.VMEM((ROUTES, inner, tiles, height, tile_cells), bf16),
            pltpu.VMEM((ROUTES, inner, tiles, height, tile_cells), bf16),
        ]
        + [pltpu.VMEM((cap + 1, height, tile_cells), bf16)] * leaves
        + [
            pltpu.SemaphoreType.DMA((messages,)),
            pltpu.SemaphoreType.DMA((messages,)),
            pltpu.SemaphoreType.DMA((CHUNKS,)),
            pltpu.SemaphoreType.DMA((writers,)),
            pltpu.SemaphoreType.DMA((len(STEPS) + 1,)),
            pltpu.SemaphoreType.DMA,
        ],
        compiler_params=pltpu.CompilerParams(
            collective_id=0, has_side_effects=True, vmem_limit_bytes=52 * 1024 * 1024
        ),
        cost_estimate=pl.CostEstimate(flops=1208000000, bytes_accessed=19700000, transcendentals=0),
    )(ints, fields, weights)


def solution(mesh):
    placed = (
        P("face", None, "blk"),
        P(("face", "blk"), None, None, None, None),
        P(("face", "blk"), None, None),
        P(("face", "blk"), None, None),
        P(("face", "blk"), None),
    )
    return jax.shard_map(
        on_device,
        mesh=mesh,
        in_specs=placed,
        out_specs=P(("face", "blk"), None, None),
        check_vma=False,
    )
```

```python
import jax
import jax.numpy as jnp
from jax import lax
from jax.experimental import pallas as pl
from jax.experimental.pallas import tpu as pltpu
from jax.sharding import PartitionSpec as P

MESH = pl.DeviceIdType.MESH
SIDE = 4
CHUNKS = 8
ROUTES = 2
PARTS = 2
STEPS = {"x+": (1, 0), "x-": (3, 0), "y+": (0, 1), "y-": (0, 3)}
TREES = (
    {
        (0, 1): "y-", (0, 2): "y+", (0, 3): "y+", (1, 0): "x-", (1, 1): "x-",
        (1, 2): "y-", (1, 3): "x-", (2, 0): "y+", (2, 1): "x-", (2, 2): "y-",
        (2, 3): "x+", (3, 0): "x+", (3, 1): "x+", (3, 2): "y+", (3, 3): "x+",
    },
    {
        (0, 1): "y-", (0, 2): "x+", (0, 3): "y+", (1, 0): "x-", (1, 1): "y-",
        (1, 2): "y-", (1, 3): "y+", (2, 0): "x+", (2, 1): "x-", (2, 2): "x-",
        (2, 3): "x+", (3, 0): "x+", (3, 1): "y-", (3, 2): "y+", (3, 3): "y+",
    },
)
PLAN = (
    ((2, 0), ()),
    ((2, 2), ()),
    ((0, 2), ()),
    ((2, 1), ()),
    ((3, 1), ()),
    ((3, 2), ((0, (2, 1), 0), (0, (2, 1), 1),)),
    ((1, 2), ((1, (1, 2), 0), (1, (1, 2), 1),)),
    ((2, 3), ()),
    ((1, 3), ()),
    ((3, 3), ()),
    ((0, 3), ()),
    ((1, 1), (
        (0, (1, 1), 0), (0, (3, 3), 0), (1, (1, 1), 0), (0, (1, 1), 1),
        (0, (3, 3), 1),
    )),
    ((1, 0), (
        (1, (3, 3), 0), (1, (3, 3), 1), (1, (1, 1), 1),
    )),
    ((3, 0), ()),
    ((0, 1), (
        (0, (0, 1), 0), (0, (0, 3), 0), (1, (1, 0), 0),
    )),
    ((0, 0), (
        (1, (3, 0), 0), (0, (0, 1), 1), (0, (0, 3), 1), (1, (1, 0), 1),
        (1, (3, 0), 1), (0, (0, 0), 0), (1, (0, 0), 0),
    )),
)
LAST = (
    (0, (0, 3), 0), (1, (1, 0), 0), (1, (3, 0), 0), (0, (0, 1), 0),
    (0, (0, 3), 1), (1, (1, 0), 1), (1, (3, 0), 1), (0, (0, 1), 1),
)
TABLES_AFTER = 4
ORDER = tuple(entry[0] for entry in PLAN)


def parent(route, o):
    dx, dy = STEPS[TREES[route][o]]
    return ((o[0] + dx) % SIDE, (o[1] + dy) % SIDE)


def children(route, o):
    return [v for v in TREES[route] if parent(route, v) == o]


INNER = [[v for v in tree if children(route, v)] for route, tree in enumerate(TREES)]
LEAVES = [[v for v in tree if not children(route, v)] for route, tree in enumerate(TREES)]


def coded(values):
    word = sum(v << (2 * k) for k, v in enumerate(values))
    return word - (1 << 32) if word >= 1 << 31 else word


def kernel(
    ints_in, fields_ref, weights_ref, out_ref,
    ints, cells, wts, part, col_own, col_send, col_recv, turns, early, tab_send, tab_recv, tab, sums, sums_in,
    *rest,
):
    raw_in = {}
    for route in range(ROUTES):
        for v in LEAVES[route]:
            raw_in[route, v] = rest[len(raw_in)]
    send_sem, recv_sem, field_sem, weight_sem, tab_sem, ints_sem = rest[len(raw_in):]
    bx, rows, width = fields_ref.shape
    cap, writers = ints.shape[1] // 2, ints.shape[2]
    tiles = out_ref.shape[0]
    height = rows // ROUTES
    share = tiles // PARTS
    faces = lax.axis_size("face")
    face = lax.axis_index("face")
    blk = lax.axis_index("blk")
    px, py = blk // SIDE, lax.rem(blk, SIDE)

    def at(a, b):
        return lax.rem(px + a, SIDE) * SIDE + lax.rem(py + b, SIDE)

    def writer(o):
        return at((SIDE - o[0]) % SIDE, (SIDE - o[1]) % SIDE)

    fields_in = []
    step = bx // CHUNKS
    for i in range(CHUNKS):
        copy = pltpu.make_async_copy(
            fields_ref.at[pl.ds(i * step, step)], cells.at[pl.ds(1 + i * step, step)], field_sem.at[i]
        )
        copy.start()
        fields_in.append(copy)
    near = {name: (face, at(*step)) for name, step in STEPS.items()}
    up, down = lax.rem(face + 1, faces), lax.rem(face + faces - 1, faces)
    right, left = lax.rem(blk + 1, writers), lax.rem(blk + writers - 1, writers)
    barrier = pltpu.get_barrier_semaphore()
    greeted = [(up, blk), (down, blk), (face, left), (face, right)] + list(near.values())
    for peer in greeted:
        pl.semaphore_signal(barrier, inc=1, device_id=peer, device_id_type=MESH)

    ints_copy = pltpu.make_async_copy(ints_in, ints, ints_sem)
    ints_copy.start()
    weights_in = [
        pltpu.make_async_copy(weights_ref.at[0, writer(o)], wts.at[k, :, pl.ds(0, weights_ref.shape[3])], weight_sem.at[k])
        for k, o in enumerate(ORDER)
    ]

    messages = []

    def message(src, dst, peer):
        i = len(messages)
        messages.append(
            pltpu.make_async_remote_copy(
                src_ref=src, dst_ref=dst, send_sem=send_sem.at[i], recv_sem=recv_sem.at[i],
                device_id=peer, device_id_type=MESH,
            )
        )
        return messages[i]

    halo = [
        message(fields_ref.at[bx - 1], cells.at[0], (up, blk)),
        message(fields_ref.at[0], cells.at[bx + 1], (down, blk)),
        message(col_send.at[0], col_recv.at[0], (face, right)),
        message(col_send.at[1], col_recv.at[1], (face, left)),
    ]
    tables = [message(tab_send, tab_recv.at[i], near[name]) for i, name in enumerate(STEPS)]
    raw, summed = {}, {}
    for route, tree in enumerate(TREES):
        rs = pl.ds(route * height, height)
        for v in LEAVES[route]:
            raw[route, v] = message(
                part.at[ORDER.index(v), pl.ds(0, cap), rs], raw_in[route, v].at[pl.ds(0, cap)], near[tree[v]]
            )
        for i, v in enumerate(INNER[route]):
            for h in range(PARTS):
                some = pl.ds(h * share, share)
                summed[route, v, h] = message(sums.at[route, i, some], sums_in.at[route, i, some], near[tree[v]])

    depth = weights_ref.shape[3]
    group = width // cap

    def clear(k, carry):
        for c in range(cap):
            wts[k, c, pl.ds(depth, width), :] = jnp.zeros((width, wts.shape[3]), wts.dtype)
        return carry

    lax.fori_loop(0, writers, clear, 0)

    lanes = lax.broadcasted_iota(jnp.int32, (rows, width), 1)

    def pack_edges():
        edges = (jnp.zeros((rows, width), jnp.float32), jnp.zeros((rows, width), jnp.float32))
        for i in range(CHUNKS):
            fields_in[i].wait()
            if i >= CHUNKS // 2:
                weights_in[i - CHUNKS // 2].start()

            def pick(j, edges):
                x = i * step + j
                turned = pltpu.roll(cells[1 + x], lax.rem(x + 1, width), 1)
                return (
                    jnp.where(lanes == x, turned, edges[0]),
                    jnp.where(lanes == lax.rem(x + 1, width), turned, edges[1]),
                )

            edges = lax.fori_loop(0, step, pick, edges, unroll=4)
        for i in range(2):
            col_own[i] = edges[i]
            col_send[i] = edges[i].astype(col_send.dtype)

    core = lax.rem(face, 2)
    pl.when(core == 0)(pack_edges)
    pl.semaphore_wait(barrier, len(greeted))
    halo[0].start()
    halo[1].start()
    pl.when(core != 0)(pack_edges)
    halo[2].start()
    halo[3].start()
    for copy in weights_in[CHUNKS - CHUNKS // 2:]:
        copy.start()

    ints_copy.wait()
    lane = lax.broadcasted_iota(jnp.int32, (1, 128), 1)

    def make_row(d, carry):
        row = jnp.full((1, 128), cap, jnp.int32)
        for c in range(cap):
            target = jnp.where(c < ints[0, 2 * cap, d], ints[0, cap + c, d], 127)
            row = jnp.where(lane == target, c, row)
        tab_send[pl.ds(d, 1), :] = row
        return carry

    lax.fori_loop(0, writers, make_row, 0)
    for copy in tables:
        copy.start()
    for buf in raw_in.values():
        buf[cap] = jnp.zeros((height, width), buf.dtype)
    for k, o in enumerate(ORDER):
        if o not in LEAVES[0] or o not in LEAVES[1]:
            part[k, cap] = jnp.zeros((rows, width), part.dtype)
    group_row = lax.broadcasted_iota(jnp.int32, (group, wts.shape[3]), 0)
    turn_row = lax.broadcasted_iota(jnp.int32, (2 * width, width), 0)
    code_x = jnp.int32(coded([(SIDE - o[0]) % SIDE for o in ORDER]))
    code_y = jnp.int32(coded([(SIDE - o[1]) % SIDE for o in ORDER]))

    def writer_at(k):
        return at((code_x >> (2 * k)) & 3, (code_y >> (2 * k)) & 3)

    def stack(x):
        value = cells[x + 1]
        grad_x = cells[x + 2] - cells[x]
        grad_y = pltpu.roll(value, width - 1, 1) - pltpu.roll(value, 1, 1)
        return jnp.concatenate([value + value, grad_x, grad_y], axis=1).astype(jnp.bfloat16)

    def pick_edges(d):
        where_from = jnp.full((1, width), -1, jnp.int32)
        for c in range(cap):
            x = ints[0, c, d]
            where_from = jnp.where(lane == c * group, x, where_from)
            where_from = jnp.where(lane == c * group + group - 1, width + lax.rem(x + 1, width), where_from)
        return jnp.where(turn_row == where_from, 1.0, 0.0).astype(jnp.bfloat16)

    def turn(picked):
        return jnp.dot(turns[...], picked, preferred_element_type=jnp.float32).astype(jnp.bfloat16)

    def edge_rows(k):
        for c in range(cap):
            first = wts[k, c, pl.ds(2 * width, group), :].astype(jnp.float32)
            final = wts[k, c, pl.ds(3 * width - group, group), :].astype(jnp.float32)
            edge = jnp.where(group_row == 0, first, jnp.where(group_row == group - 1, final, 0.0))
            wts[k, c, pl.ds(depth + c * group, group), :] = edge.astype(wts.dtype)

    halo[0].wait_recv()
    halo[1].wait_recv()
    weights_in[0].wait()
    edge_rows(0)
    d_first = writer(ORDER[0])

    def begin(c, carry):
        early[c] = jnp.dot(stack(ints[0, c, d_first]), wts[0, c, pl.ds(0, depth), :], preferred_element_type=jnp.float32)
        return carry

    lax.fori_loop(0, cap, begin, 0, unroll=4)
    picked = pick_edges(d_first)
    halo[2].wait_recv()
    halo[3].wait_recv()
    turns[:, pl.ds(0, width)] = (col_own[0] - col_recv[0].astype(jnp.float32)).astype(turns.dtype)
    turns[:, pl.ds(width, width)] = (col_recv[1].astype(jnp.float32) - col_own[1]).astype(turns.dtype)
    turned = turn(picked)
    for c in range(cap):
        product = early[c] + jnp.dot(turned, wts[0, c, pl.ds(depth, width), :], preferred_element_type=jnp.float32)
        part[0, c] = product.astype(part.dtype)
    for route in range(ROUTES):
        if ORDER[0] in LEAVES[route]:
            raw[route, ORDER[0]].start()

    def read_tables():
        for copy in tables:
            copy.wait_recv()
        sources = [tab_recv.at[i] for i in range(len(STEPS))] + [tab_send]
        copies = [pltpu.make_async_copy(src, tab.at[i], tab_sem.at[i]) for i, src in enumerate(sources)]
        for copy in copies:
            copy.start()
        for copy in copies:
            copy.wait()

    here = set()

    def gather(route, o, h, store):
        d = writer(o)
        k = ORDER.index(o)
        rs = pl.ds(route * height, height)
        below = children(route, o)
        plain = [v for v in below if v in LEAVES[route]]
        dense = [INNER[route].index(v) for v in below if v in INNER[route]]
        if o == (0, 0):
            dense = []
        for v in plain:
            if (route, v) not in here:
                raw[route, v].wait_recv()
                here.add((route, v))
        for i in dense:
            summed[route, INNER[route][i], h].wait_recv()
        ways = list(STEPS)

        def one(j, carry):
            t = h * share + j
            total = part[k, tab[len(ways), d, t], rs, :].astype(jnp.float32)
            for v in plain:
                slot = tab[ways.index(TREES[route][v]), d, t]
                total += raw_in[route, v][slot].astype(jnp.float32)
            for i in dense:
                total += sums_in[route, i, t].astype(jnp.float32)
            store(t, total)
            return carry

        lax.fori_loop(0, share, one, 0, unroll=8)

    def follow(route, o, h):
        if o == (0, 0):
            def store(t, total):
                out_ref[t, pl.ds(route * height, height), :] = total * 0.5

            for part_of in range(PARTS):
                gather(route, o, part_of, store)
        else:
            i = INNER[route].index(o)

            def store(t, total):
                sums[route, i, t] = total.astype(sums.dtype)

            gather(route, o, h, store)
            summed[route, o, h].start()

    def products(k, turned):
        d = writer_at(k)
        pltpu.make_async_copy(weights_ref.at[0, 0], wts.at[k, :, pl.ds(0, depth)], weight_sem.at[k]).wait()
        edge_rows(k)
        later = turn(pick_edges(writer_at(lax.rem(k + 1, len(PLAN)))))
        for c in range(cap):
            stacked = jnp.concatenate([stack(ints[0, c, d]), turned], axis=1)
            product = jnp.dot(stacked, wts[k, c], preferred_element_type=jnp.float32)
            part[k, c] = product.astype(part.dtype)

        for i, (o, sums_after) in enumerate(PLAN):
            if i == 0:
                continue
            ready = [raw[route, o] for route in range(ROUTES) if o in LEAVES[route]]
            if i == len(PLAN) - 1:
                sums_after = ()
            if ready or sums_after or i == TABLES_AFTER:
                @pl.when(k == i)
                def _():
                    for copy in ready:
                        copy.start()
                    if i == TABLES_AFTER:
                        read_tables()
                    for entry in sums_after:
                        follow(*entry)
        return later

    lax.fori_loop(1, len(PLAN), products, turn(pick_edges(writer(ORDER[1]))))
    for entry in PLAN[-1][1]:
        follow(*entry)
    for route, v, h in LAST:
        rs = pl.ds(route * height, height)
        i = INNER[route].index(v)
        summed[route, v, h].wait_recv()

        def add(j, carry):
            t = h * share + j
            out_ref[t, rs, :] += sums_in[route, i, t].astype(jnp.float32) * 0.5
            return carry

        lax.fori_loop(0, share, add, 0, unroll=8)
    for copy in messages:
        copy.wait_send()


def on_device(fields, weights, src_tile, tgt_tile, counts):
    bx, rows, width = fields.shape
    _, writers, cap, depth, tile_cells = weights.shape
    tiles = 16
    height = rows // ROUTES
    leaves = sum(len(some) for some in LEAVES)
    inner = len(INNER[0])
    messages = 8 + leaves + ROUTES * inner * PARTS
    bf16 = jnp.bfloat16
    ints = jnp.concatenate(
        [jnp.swapaxes(src_tile, 1, 2), jnp.swapaxes(tgt_tile, 1, 2), counts[:, None, :]], axis=1
    )
    return pl.pallas_call(
        kernel,
        out_shape=jax.ShapeDtypeStruct((tiles, rows, tile_cells), jnp.float32),
        in_specs=[pl.BlockSpec(memory_space=pl.ANY)] * 3,
        out_specs=pl.BlockSpec(memory_space=pltpu.VMEM),
        scratch_shapes=[
            pltpu.SMEM((1, 2 * cap + 1, writers), jnp.int32),
            pltpu.VMEM((bx + 2, rows, width), jnp.float32),
            pltpu.VMEM((writers, cap, depth + width, tile_cells), bf16),
            pltpu.VMEM((writers, cap + 1, rows, tile_cells), bf16),
            pltpu.VMEM((2, rows, width), jnp.float32),
            pltpu.VMEM((2, rows, width), bf16),
            pltpu.VMEM((2, rows, width), bf16),
            pltpu.VMEM((rows, 2 * width), bf16),
            pltpu.VMEM((cap, rows, tile_cells), jnp.float32),
            pltpu.VMEM((writers, 128), jnp.int32),
            pltpu.VMEM((len(STEPS), writers, 128), jnp.int32),
            pltpu.SMEM((len(STEPS) + 1, writers, 128), jnp.int32),
            pltpu.VMEM((ROUTES, inner, tiles, height, tile_cells), bf16),
            pltpu.VMEM((ROUTES, inner, tiles, height, tile_cells), bf16),
        ]
        + [pltpu.VMEM((cap + 1, height, tile_cells), bf16)] * leaves
        + [
            pltpu.SemaphoreType.DMA((messages,)),
            pltpu.SemaphoreType.DMA((messages,)),
            pltpu.SemaphoreType.DMA((CHUNKS,)),
            pltpu.SemaphoreType.DMA((writers,)),
            pltpu.SemaphoreType.DMA((len(STEPS) + 1,)),
            pltpu.SemaphoreType.DMA,
        ],
        compiler_params=pltpu.CompilerParams(
            collective_id=0, has_side_effects=True, vmem_limit_bytes=52 * 1024 * 1024
        ),
        cost_estimate=pl.CostEstimate(flops=1208000000, bytes_accessed=19700000, transcendentals=0),
    )(ints, fields, weights)


def solution(mesh):
    placed = (
        P("face", None, "blk"),
        P(("face", "blk"), None, None, None, None),
        P(("face", "blk"), None, None),
        P(("face", "blk"), None, None),
        P(("face", "blk"), None),
    )
    return jax.shard_map(
        on_device,
        mesh=mesh,
        in_specs=placed,
        out_specs=P(("face", "blk"), None, None),
        check_vma=False,
    )
```

```python
import jax
import jax.numpy as jnp
from jax import lax
from jax.experimental import pallas as pl
from jax.experimental.pallas import tpu as pltpu
from jax.sharding import PartitionSpec as P

MESH = pl.DeviceIdType.MESH
SIDE = 4
CHUNKS = 8
ROUTES = 2
PARTS = 2
STEPS = {"x+": (1, 0), "x-": (3, 0), "y+": (0, 1), "y-": (0, 3)}
TREES = (
    {
        (0, 1): "y-", (0, 2): "y+", (0, 3): "y+", (1, 0): "x-", (1, 1): "x-",
        (1, 2): "y-", (1, 3): "x-", (2, 0): "y+", (2, 1): "x-", (2, 2): "y-",
        (2, 3): "x+", (3, 0): "x+", (3, 1): "x+", (3, 2): "y+", (3, 3): "x+",
    },
    {
        (0, 1): "y-", (0, 2): "x+", (0, 3): "y+", (1, 0): "x-", (1, 1): "y-",
        (1, 2): "y-", (1, 3): "y+", (2, 0): "x+", (2, 1): "x-", (2, 2): "x-",
        (2, 3): "x+", (3, 0): "x+", (3, 1): "y-", (3, 2): "y+", (3, 3): "y+",
    },
)
PLAN = (
    ((2, 0), ()),
    ((2, 2), ()),
    ((0, 2), ()),
    ((2, 1), ()),
    ((3, 1), ()),
    ((3, 2), ((0, (2, 1), 0), (0, (2, 1), 1),)),
    ((1, 2), ((1, (1, 2), 0), (1, (1, 2), 1),)),
    ((2, 3), ()),
    ((1, 3), ()),
    ((3, 3), ()),
    ((0, 3), ()),
    ((1, 1), (
        (0, (1, 1), 0), (0, (3, 3), 0), (1, (1, 1), 0), (0, (1, 1), 1),
        (0, (3, 3), 1),
    )),
    ((1, 0), (
        (1, (3, 3), 0), (1, (3, 3), 1), (1, (1, 1), 1),
    )),
    ((3, 0), ()),
    ((0, 1), (
        (0, (0, 1), 0), (0, (0, 3), 0), (1, (1, 0), 0),
    )),
    ((0, 0), (
        (1, (3, 0), 0), (0, (0, 1), 1), (0, (0, 3), 1), (1, (1, 0), 1),
        (1, (3, 0), 1), (0, (0, 0), 0), (1, (0, 0), 0),
    )),
)
LAST = (
    (0, (0, 3), 0), (1, (1, 0), 0), (1, (3, 0), 0), (0, (0, 1), 0),
    (0, (0, 3), 1), (1, (1, 0), 1), (1, (3, 0), 1), (0, (0, 1), 1),
)
TABLES_AFTER = 4
ORDER = tuple(entry[0] for entry in PLAN)


def parent(route, o):
    dx, dy = STEPS[TREES[route][o]]
    return ((o[0] + dx) % SIDE, (o[1] + dy) % SIDE)


def children(route, o):
    return [v for v in TREES[route] if parent(route, v) == o]


INNER = [[v for v in tree if children(route, v)] for route, tree in enumerate(TREES)]
LEAVES = [[v for v in tree if not children(route, v)] for route, tree in enumerate(TREES)]


def coded(values):
    word = sum(v << (2 * k) for k, v in enumerate(values))
    return word - (1 << 32) if word >= 1 << 31 else word


def kernel(
    ints_in, fields_ref, weights_ref, out_ref,
    ints, cells, wts, part, col_own, col_send, col_recv, turns, early, tab_send, tab_recv, tab, sums, sums_in,
    *rest,
):
    raw_in = {}
    for route in range(ROUTES):
        for v in LEAVES[route]:
            raw_in[route, v] = rest[len(raw_in)]
    send_sem, recv_sem, field_sem, weight_sem, tab_sem, ints_sem = rest[len(raw_in):]
    bx, rows, width = fields_ref.shape
    cap, writers = ints.shape[1] // 2, ints.shape[2]
    tiles = out_ref.shape[0]
    height = rows // ROUTES
    share = tiles // PARTS
    faces = lax.axis_size("face")
    face = lax.axis_index("face")
    blk = lax.axis_index("blk")
    px, py = blk // SIDE, lax.rem(blk, SIDE)

    def at(a, b):
        return lax.rem(px + a, SIDE) * SIDE + lax.rem(py + b, SIDE)

    def writer(o):
        return at((SIDE - o[0]) % SIDE, (SIDE - o[1]) % SIDE)

    fields_in = []
    step = bx // CHUNKS
    for i in range(CHUNKS):
        copy = pltpu.make_async_copy(
            fields_ref.at[pl.ds(i * step, step)], cells.at[pl.ds(1 + i * step, step)], field_sem.at[i]
        )
        copy.start()
        fields_in.append(copy)
    near = {name: (face, at(*step)) for name, step in STEPS.items()}
    up, down = lax.rem(face + 1, faces), lax.rem(face + faces - 1, faces)
    right, left = lax.rem(blk + 1, writers), lax.rem(blk + writers - 1, writers)
    barrier = pltpu.get_barrier_semaphore()
    greeted = [(up, blk), (down, blk), (face, left), (face, right)] + list(near.values())
    for peer in greeted:
        pl.semaphore_signal(barrier, inc=1, device_id=peer, device_id_type=MESH)

    ints_copy = pltpu.make_async_copy(ints_in, ints, ints_sem)
    ints_copy.start()
    weights_in = [
        pltpu.make_async_copy(weights_ref.at[0, writer(o)], wts.at[k, :, pl.ds(0, weights_ref.shape[3])], weight_sem.at[k])
        for k, o in enumerate(ORDER)
    ]

    messages = []

    def message(src, dst, peer):
        i = len(messages)
        messages.append(
            pltpu.make_async_remote_copy(
                src_ref=src, dst_ref=dst, send_sem=send_sem.at[i], recv_sem=recv_sem.at[i],
                device_id=peer, device_id_type=MESH,
            )
        )
        return messages[i]

    halo = [
        message(fields_ref.at[bx - 1], cells.at[0], (up, blk)),
        message(fields_ref.at[0], cells.at[bx + 1], (down, blk)),
        message(col_send.at[0], col_recv.at[0], (face, right)),
        message(col_send.at[1], col_recv.at[1], (face, left)),
    ]
    tables = [message(tab_send, tab_recv.at[i], near[name]) for i, name in enumerate(STEPS)]
    raw, summed = {}, {}
    for route, tree in enumerate(TREES):
        rs = pl.ds(route * height, height)
        for v in LEAVES[route]:
            raw[route, v] = message(
                part.at[ORDER.index(v), pl.ds(0, cap), rs], raw_in[route, v].at[pl.ds(0, cap)], near[tree[v]]
            )
        for i, v in enumerate(INNER[route]):
            for h in range(PARTS):
                some = pl.ds(h * share, share)
                summed[route, v, h] = message(sums.at[route, i, some], sums_in.at[route, i, some], near[tree[v]])

    depth = weights_ref.shape[3]
    group = width // cap

    def clear(k, carry):
        for c in range(cap):
            wts[k, c, pl.ds(depth, width), :] = jnp.zeros((width, wts.shape[3]), wts.dtype)
        return carry

    def clear_all():
        lax.fori_loop(0, writers, clear, 0)

    lanes = lax.broadcasted_iota(jnp.int32, (rows, width), 1)
    lane = lax.broadcasted_iota(jnp.int32, (1, 128), 1)

    def make_tables():
        ints_copy.wait()

        def make_row(d, carry):
            row = jnp.full((1, 128), cap, jnp.int32)
            for c in range(cap):
                target = jnp.where(c < ints[0, 2 * cap, d], ints[0, cap + c, d], 127)
                row = jnp.where(lane == target, c, row)
            tab_send[pl.ds(d, 1), :] = row
            return carry

        lax.fori_loop(0, writers, make_row, 0)
        for buf in raw_in.values():
            buf[cap] = jnp.zeros((height, width), buf.dtype)
        for k, o in enumerate(ORDER):
            if o not in LEAVES[0] or o not in LEAVES[1]:
                part[k, cap] = jnp.zeros((rows, width), part.dtype)

    def pack_edges():
        edges = (jnp.zeros((rows, width), jnp.float32), jnp.zeros((rows, width), jnp.float32))
        for i in range(CHUNKS):
            fields_in[i].wait()
            if i == CHUNKS - 1:
                weights_in[0].start()

            def pick(j, edges):
                x = i * step + j
                turned = pltpu.roll(cells[1 + x], lax.rem(x + 1, width), 1)
                return (
                    jnp.where(lanes == x, turned, edges[0]),
                    jnp.where(lanes == lax.rem(x + 1, width), turned, edges[1]),
                )

            edges = lax.fori_loop(0, step, pick, edges, unroll=4)
        for i in range(2):
            col_own[i] = edges[i]
            col_send[i] = edges[i].astype(col_send.dtype)

    core = lax.rem(face, 2)

    @pl.when(core == 0)
    def _():
        make_tables()
        clear_all()
        pack_edges()

    pl.semaphore_wait(barrier, len(greeted))
    halo[0].start()
    halo[1].start()

    @pl.when(core != 0)
    def _():
        make_tables()
        pack_edges()

    halo[2].start()
    halo[3].start()
    for copy in weights_in[1:]:
        copy.start()
    for copy in tables:
        copy.start()
    pl.when(core != 0)(clear_all)

    group_row = lax.broadcasted_iota(jnp.int32, (group, wts.shape[3]), 0)
    turn_row = lax.broadcasted_iota(jnp.int32, (2 * width, width), 0)
    code_x = jnp.int32(coded([(SIDE - o[0]) % SIDE for o in ORDER]))
    code_y = jnp.int32(coded([(SIDE - o[1]) % SIDE for o in ORDER]))

    def writer_at(k):
        return at((code_x >> (2 * k)) & 3, (code_y >> (2 * k)) & 3)

    def stack(x):
        value = cells[x + 1]
        grad_x = cells[x + 2] - cells[x]
        grad_y = pltpu.roll(value, width - 1, 1) - pltpu.roll(value, 1, 1)
        return jnp.concatenate([value + value, grad_x, grad_y], axis=1).astype(jnp.bfloat16)

    def pick_edges(d):
        where_from = jnp.full((1, width), -1, jnp.int32)
        for c in range(cap):
            x = ints[0, c, d]
            where_from = jnp.where(lane == c * group, x, where_from)
            where_from = jnp.where(lane == c * group + group - 1, width + lax.rem(x + 1, width), where_from)
        return jnp.where(turn_row == where_from, 1.0, 0.0).astype(jnp.bfloat16)

    def turn(picked):
        return jnp.dot(turns[...], picked, preferred_element_type=jnp.float32).astype(jnp.bfloat16)

    def edge_rows(k):
        for c in range(cap):
            first = wts[k, c, pl.ds(2 * width, group), :].astype(jnp.float32)
            final = wts[k, c, pl.ds(3 * width - group, group), :].astype(jnp.float32)
            edge = jnp.where(group_row == 0, first, jnp.where(group_row == group - 1, final, 0.0))
            wts[k, c, pl.ds(depth + c * group, group), :] = edge.astype(wts.dtype)

    halo[0].wait_recv()
    halo[1].wait_recv()
    weights_in[0].wait()
    edge_rows(0)
    d_first = writer(ORDER[0])

    def begin(c, carry):
        early[c] = jnp.dot(stack(ints[0, c, d_first]), wts[0, c, pl.ds(0, depth), :], preferred_element_type=jnp.float32)
        return carry

    lax.fori_loop(0, cap, begin, 0, unroll=4)
    picked = pick_edges(d_first)
    halo[2].wait_recv()
    halo[3].wait_recv()
    turns[:, pl.ds(0, width)] = (col_own[0] - col_recv[0].astype(jnp.float32)).astype(turns.dtype)
    turns[:, pl.ds(width, width)] = (col_recv[1].astype(jnp.float32) - col_own[1]).astype(turns.dtype)
    turned = turn(picked)
    for c in range(cap):
        product = early[c] + jnp.dot(turned, wts[0, c, pl.ds(depth, width), :], preferred_element_type=jnp.float32)
        part[0, c] = product.astype(part.dtype)
    for route in range(ROUTES):
        if ORDER[0] in LEAVES[route]:
            raw[route, ORDER[0]].start()

    def read_tables():
        for copy in tables:
            copy.wait_recv()
        sources = [tab_recv.at[i] for i in range(len(STEPS))] + [tab_send]
        copies = [pltpu.make_async_copy(src, tab.at[i], tab_sem.at[i]) for i, src in enumerate(sources)]
        for copy in copies:
            copy.start()
        for copy in copies:
            copy.wait()

    here = set()

    def gather(route, o, h, store):
        d = writer(o)
        k = ORDER.index(o)
        rs = pl.ds(route * height, height)
        below = children(route, o)
        plain = [v for v in below if v in LEAVES[route]]
        dense = [INNER[route].index(v) for v in below if v in INNER[route]]
        if o == (0, 0):
            dense = []
        for v in plain:
            if (route, v) not in here:
                raw[route, v].wait_recv()
                here.add((route, v))
        for i in dense:
            summed[route, INNER[route][i], h].wait_recv()
        ways = list(STEPS)

        def one(j, carry):
            t = h * share + j
            total = part[k, tab[len(ways), d, t], rs, :].astype(jnp.float32)
            for v in plain:
                slot = tab[ways.index(TREES[route][v]), d, t]
                total += raw_in[route, v][slot].astype(jnp.float32)
            for i in dense:
                total += sums_in[route, i, t].astype(jnp.float32)
            store(t, total)
            return carry

        lax.fori_loop(0, share, one, 0, unroll=8)

    def follow(route, o, h):
        if o == (0, 0):
            def store(t, total):
                out_ref[t, pl.ds(route * height, height), :] = total * 0.5

            for part_of in range(PARTS):
                gather(route, o, part_of, store)
        else:
            i = INNER[route].index(o)

            def store(t, total):
                sums[route, i, t] = total.astype(sums.dtype)

            gather(route, o, h, store)
            summed[route, o, h].start()

    def products(k, turned):
        d = writer_at(k)
        pltpu.make_async_copy(weights_ref.at[0, 0], wts.at[k, :, pl.ds(0, depth)], weight_sem.at[k]).wait()
        edge_rows(k)
        later = turn(pick_edges(writer_at(lax.rem(k + 1, len(PLAN)))))
        for c in range(cap):
            stacked = jnp.concatenate([stack(ints[0, c, d]), turned], axis=1)
            product = jnp.dot(stacked, wts[k, c], preferred_element_type=jnp.float32)
            part[k, c] = product.astype(part.dtype)

        for i, (o, sums_after) in enumerate(PLAN):
            if i == 0:
                continue
            ready = [raw[route, o] for route in range(ROUTES) if o in LEAVES[route]]
            if i == len(PLAN) - 1:
                sums_after = ()
            if ready or sums_after or i == TABLES_AFTER:
                @pl.when(k == i)
                def _():
                    for copy in ready:
                        copy.start()
                    if i == TABLES_AFTER:
                        read_tables()
                    for entry in sums_after:
                        follow(*entry)
        return later

    lax.fori_loop(1, len(PLAN), products, turn(pick_edges(writer(ORDER[1]))))
    for entry in PLAN[-1][1]:
        follow(*entry)
    for route, v, h in LAST:
        rs = pl.ds(route * height, height)
        i = INNER[route].index(v)
        summed[route, v, h].wait_recv()

        def add(j, carry):
            t = h * share + j
            out_ref[t, rs, :] += sums_in[route, i, t].astype(jnp.float32) * 0.5
            return carry

        lax.fori_loop(0, share, add, 0, unroll=8)
    for copy in messages:
        copy.wait_send()


def on_device(fields, weights, src_tile, tgt_tile, counts):
    bx, rows, width = fields.shape
    _, writers, cap, depth, tile_cells = weights.shape
    tiles = 16
    height = rows // ROUTES
    leaves = sum(len(some) for some in LEAVES)
    inner = len(INNER[0])
    messages = 8 + leaves + ROUTES * inner * PARTS
    bf16 = jnp.bfloat16
    ints = jnp.concatenate(
        [jnp.swapaxes(src_tile, 1, 2), jnp.swapaxes(tgt_tile, 1, 2), counts[:, None, :]], axis=1
    )
    return pl.pallas_call(
        kernel,
        out_shape=jax.ShapeDtypeStruct((tiles, rows, tile_cells), jnp.float32),
        in_specs=[pl.BlockSpec(memory_space=pl.ANY)] * 3,
        out_specs=pl.BlockSpec(memory_space=pltpu.VMEM),
        scratch_shapes=[
            pltpu.SMEM((1, 2 * cap + 1, writers), jnp.int32),
            pltpu.VMEM((bx + 2, rows, width), jnp.float32),
            pltpu.VMEM((writers, cap, depth + width, tile_cells), bf16),
            pltpu.VMEM((writers, cap + 1, rows, tile_cells), bf16),
            pltpu.VMEM((2, rows, width), jnp.float32),
            pltpu.VMEM((2, rows, width), bf16),
            pltpu.VMEM((2, rows, width), bf16),
            pltpu.VMEM((rows, 2 * width), bf16),
            pltpu.VMEM((cap, rows, tile_cells), jnp.float32),
            pltpu.VMEM((writers, 128), jnp.int32),
            pltpu.VMEM((len(STEPS), writers, 128), jnp.int32),
            pltpu.SMEM((len(STEPS) + 1, writers, 128), jnp.int32),
            pltpu.VMEM((ROUTES, inner, tiles, height, tile_cells), bf16),
            pltpu.VMEM((ROUTES, inner, tiles, height, tile_cells), bf16),
        ]
        + [pltpu.VMEM((cap + 1, height, tile_cells), bf16)] * leaves
        + [
            pltpu.SemaphoreType.DMA((messages,)),
            pltpu.SemaphoreType.DMA((messages,)),
            pltpu.SemaphoreType.DMA((CHUNKS,)),
            pltpu.SemaphoreType.DMA((writers,)),
            pltpu.SemaphoreType.DMA((len(STEPS) + 1,)),
            pltpu.SemaphoreType.DMA,
        ],
        compiler_params=pltpu.CompilerParams(
            collective_id=0, has_side_effects=True, vmem_limit_bytes=52 * 1024 * 1024
        ),
        cost_estimate=pl.CostEstimate(flops=1208000000, bytes_accessed=19700000, transcendentals=0),
    )(ints, fields, weights)


def solution(mesh):
    placed = (
        P("face", None, "blk"),
        P(("face", "blk"), None, None, None, None),
        P(("face", "blk"), None, None),
        P(("face", "blk"), None, None),
        P(("face", "blk"), None),
    )
    return jax.shard_map(
        on_device,
        mesh=mesh,
        in_specs=placed,
        out_specs=P(("face", "blk"), None, None),
        check_vma=False,
    )
```

```python
import jax
import jax.numpy as jnp
from jax import lax
from jax.experimental import pallas as pl
from jax.experimental.pallas import tpu as pltpu
from jax.sharding import PartitionSpec as P

MESH = pl.DeviceIdType.MESH
SIDE = 4
CHUNKS = 8
ROUTES = 2
PARTS = 2
STEPS = {"x+": (1, 0), "x-": (3, 0), "y+": (0, 1), "y-": (0, 3)}
TREES = (
    {
        (0, 1): "y-", (0, 2): "y+", (0, 3): "y+", (1, 0): "x-", (1, 1): "x-",
        (1, 2): "y-", (1, 3): "x-", (2, 0): "y+", (2, 1): "x-", (2, 2): "y-",
        (2, 3): "x+", (3, 0): "x+", (3, 1): "x+", (3, 2): "y+", (3, 3): "x+",
    },
    {
        (0, 1): "y-", (0, 2): "x+", (0, 3): "y+", (1, 0): "x-", (1, 1): "y-",
        (1, 2): "y-", (1, 3): "y+", (2, 0): "x+", (2, 1): "x-", (2, 2): "x-",
        (2, 3): "x+", (3, 0): "x+", (3, 1): "y-", (3, 2): "y+", (3, 3): "y+",
    },
)
PLAN = (
    ((2, 0), ()),
    ((2, 2), ()),
    ((0, 2), ()),
    ((2, 1), ()),
    ((3, 1), ()),
    ((3, 2), ((0, (2, 1), 0), (0, (2, 1), 1),)),
    ((1, 2), ((1, (1, 2), 0), (1, (1, 2), 1),)),
    ((2, 3), ()),
    ((1, 3), ()),
    ((3, 3), ()),
    ((0, 3), ()),
    ((1, 1), (
        (0, (1, 1), 0), (0, (3, 3), 0), (1, (1, 1), 0), (0, (1, 1), 1),
        (0, (3, 3), 1),
    )),
    ((1, 0), (
        (1, (3, 3), 0), (1, (3, 3), 1), (1, (1, 1), 1),
    )),
    ((3, 0), ()),
    ((0, 1), (
        (0, (0, 1), 0), (0, (0, 3), 0), (1, (1, 0), 0),
    )),
    ((0, 0), (
        (1, (3, 0), 0), (0, (0, 1), 1), (0, (0, 3), 1), (1, (1, 0), 1),
        (1, (3, 0), 1), (0, (0, 0), 0), (1, (0, 0), 0),
    )),
)
LAST = (
    (0, (0, 3), 0), (1, (1, 0), 0), (1, (3, 0), 0), (0, (0, 1), 0),
    (0, (0, 3), 1), (1, (1, 0), 1), (1, (3, 0), 1), (0, (0, 1), 1),
)
TABLES_AFTER = 4
ORDER = tuple(entry[0] for entry in PLAN)


def parent(route, o):
    dx, dy = STEPS[TREES[route][o]]
    return ((o[0] + dx) % SIDE, (o[1] + dy) % SIDE)


def children(route, o):
    return [v for v in TREES[route] if parent(route, v) == o]


INNER = [[v for v in tree if children(route, v)] for route, tree in enumerate(TREES)]
LEAVES = [[v for v in tree if not children(route, v)] for route, tree in enumerate(TREES)]


def coded(values):
    word = sum(v << (2 * k) for k, v in enumerate(values))
    return word - (1 << 32) if word >= 1 << 31 else word


def kernel(
    ints_in, fields_ref, weights_ref, out_ref,
    ints, cells, wts, part, col_own, col_send, col_recv, turns, early, tab_send, tab_recv, tab, sums, sums_in,
    *rest,
):
    raw_in = {}
    for route in range(ROUTES):
        for v in LEAVES[route]:
            raw_in[route, v] = rest[len(raw_in)]
    send_sem, recv_sem, field_sem, weight_sem, tab_sem, ints_sem = rest[len(raw_in):]
    bx, rows, width = fields_ref.shape
    cap, writers = ints.shape[1] // 2, ints.shape[2]
    tiles = out_ref.shape[0]
    height = rows // ROUTES
    share = tiles // PARTS
    faces = lax.axis_size("face")
    face = lax.axis_index("face")
    blk = lax.axis_index("blk")
    px, py = blk // SIDE, lax.rem(blk, SIDE)

    def at(a, b):
        return lax.rem(px + a, SIDE) * SIDE + lax.rem(py + b, SIDE)

    def writer(o):
        return at((SIDE - o[0]) % SIDE, (SIDE - o[1]) % SIDE)

    fields_in = []
    step = bx // CHUNKS
    for i in range(CHUNKS):
        copy = pltpu.make_async_copy(
            fields_ref.at[pl.ds(i * step, step)], cells.at[pl.ds(1 + i * step, step)], field_sem.at[i]
        )
        copy.start()
        fields_in.append(copy)
    near = {name: (face, at(*step)) for name, step in STEPS.items()}
    up, down = lax.rem(face + 1, faces), lax.rem(face + faces - 1, faces)
    right, left = lax.rem(blk + 1, writers), lax.rem(blk + writers - 1, writers)
    barrier = pltpu.get_barrier_semaphore()
    greeted = [(up, blk), (down, blk), (face, left), (face, right)] + list(near.values())
    for peer in greeted:
        pl.semaphore_signal(barrier, inc=1, device_id=peer, device_id_type=MESH)

    ints_copy = pltpu.make_async_copy(ints_in, ints, ints_sem)
    ints_copy.start()
    weights_in = [
        pltpu.make_async_copy(weights_ref.at[0, writer(o)], wts.at[k, :, pl.ds(0, weights_ref.shape[3])], weight_sem.at[k])
        for k, o in enumerate(ORDER)
    ]

    messages = []

    def message(src, dst, peer, i=None):
        i = len(messages) if i is None else i
        copy = pltpu.make_async_remote_copy(
            src_ref=src, dst_ref=dst, send_sem=send_sem.at[i], recv_sem=recv_sem.at[i],
            device_id=peer, device_id_type=MESH,
        )
        if i == len(messages):
            messages.append(copy)
        return copy

    halo = [
        message(fields_ref.at[bx - 1], cells.at[0], (up, blk)),
        message(fields_ref.at[0], cells.at[bx + 1], (down, blk)),
        message(col_send.at[0], col_recv.at[0], (face, right)),
        message(col_send.at[1], col_recv.at[1], (face, left)),
    ]
    tables = [message(tab_send, tab_recv.at[i], near[name]) for i, name in enumerate(STEPS)]
    raw, pieces, summed = {}, {}, {}
    for route, tree in enumerate(TREES):
        rs = pl.ds(route * height, height)
        for v in LEAVES[route]:
            k = ORDER.index(v)
            i = len(messages)
            raw[route, v] = message(part.at[k, pl.ds(0, cap), rs], raw_in[route, v].at[pl.ds(0, cap)], near[tree[v]])
            pieces[route, v] = [
                message(part.at[k, pl.ds(c, 2), rs], raw_in[route, v].at[pl.ds(c, 2)], near[tree[v]], i)
                for c in range(0, cap, 2)
            ]
        for i, v in enumerate(INNER[route]):
            for h in range(PARTS):
                some = pl.ds(h * share, share)
                summed[route, v, h] = message(sums.at[route, i, some], sums_in.at[route, i, some], near[tree[v]])

    depth = weights_ref.shape[3]
    group = width // cap

    def clear(k, carry):
        for c in range(cap):
            wts[k, c, pl.ds(depth, width), :] = jnp.zeros((width, wts.shape[3]), wts.dtype)
        return carry

    lax.fori_loop(0, writers, clear, 0)

    lanes = lax.broadcasted_iota(jnp.int32, (rows, width), 1)

    def pack_edges():
        edges = (jnp.zeros((rows, width), jnp.float32), jnp.zeros((rows, width), jnp.float32))
        for i in range(CHUNKS):
            fields_in[i].wait()
            if i >= CHUNKS // 2:
                weights_in[i - CHUNKS // 2].start()

            def pick(j, edges):
                x = i * step + j
                turned = pltpu.roll(cells[1 + x], lax.rem(x + 1, width), 1)
                return (
                    jnp.where(lanes == x, turned, edges[0]),
                    jnp.where(lanes == lax.rem(x + 1, width), turned, edges[1]),
                )

            edges = lax.fori_loop(0, step, pick, edges, unroll=4)
        for i in range(2):
            col_own[i] = edges[i]
            col_send[i] = edges[i].astype(col_send.dtype)

    core = lax.rem(face, 2)
    pl.when(core == 0)(pack_edges)
    pl.semaphore_wait(barrier, len(greeted))
    halo[0].start()
    halo[1].start()
    pl.when(core != 0)(pack_edges)
    halo[2].start()
    halo[3].start()
    for copy in weights_in[CHUNKS - CHUNKS // 2:]:
        copy.start()

    ints_copy.wait()
    lane = lax.broadcasted_iota(jnp.int32, (1, 128), 1)

    def make_row(d, carry):
        row = jnp.full((1, 128), cap, jnp.int32)
        for c in range(cap):
            target = jnp.where(c < ints[0, 2 * cap, d], ints[0, cap + c, d], 127)
            row = jnp.where(lane == target, c, row)
        tab_send[pl.ds(d, 1), :] = row
        return carry

    lax.fori_loop(0, writers, make_row, 0)
    for copy in tables:
        copy.start()
    for buf in raw_in.values():
        buf[cap] = jnp.zeros((height, width), buf.dtype)
    for k, o in enumerate(ORDER):
        if o not in LEAVES[0] or o not in LEAVES[1]:
            part[k, cap] = jnp.zeros((rows, width), part.dtype)
    group_row = lax.broadcasted_iota(jnp.int32, (group, wts.shape[3]), 0)
    turn_row = lax.broadcasted_iota(jnp.int32, (2 * width, width), 0)
    code_x = jnp.int32(coded([(SIDE - o[0]) % SIDE for o in ORDER]))
    code_y = jnp.int32(coded([(SIDE - o[1]) % SIDE for o in ORDER]))

    def writer_at(k):
        return at((code_x >> (2 * k)) & 3, (code_y >> (2 * k)) & 3)

    def stack(x):
        value = cells[x + 1]
        grad_x = cells[x + 2] - cells[x]
        grad_y = pltpu.roll(value, width - 1, 1) - pltpu.roll(value, 1, 1)
        return jnp.concatenate([value + value, grad_x, grad_y], axis=1).astype(jnp.bfloat16)

    def pick_edges(d):
        where_from = jnp.full((1, width), -1, jnp.int32)
        for c in range(cap):
            x = ints[0, c, d]
            where_from = jnp.where(lane == c * group, x, where_from)
            where_from = jnp.where(lane == c * group + group - 1, width + lax.rem(x + 1, width), where_from)
        return jnp.where(turn_row == where_from, 1.0, 0.0).astype(jnp.bfloat16)

    def turn(picked):
        return jnp.dot(turns[...], picked, preferred_element_type=jnp.float32).astype(jnp.bfloat16)

    def edge_rows(k):
        for c in range(cap):
            first = wts[k, c, pl.ds(2 * width, group), :].astype(jnp.float32)
            final = wts[k, c, pl.ds(3 * width - group, group), :].astype(jnp.float32)
            edge = jnp.where(group_row == 0, first, jnp.where(group_row == group - 1, final, 0.0))
            wts[k, c, pl.ds(depth + c * group, group), :] = edge.astype(wts.dtype)

    halo[0].wait_recv()
    halo[1].wait_recv()
    weights_in[0].wait()
    edge_rows(0)
    d_first = writer(ORDER[0])

    def begin(c, carry):
        early[c] = jnp.dot(stack(ints[0, c, d_first]), wts[0, c, pl.ds(0, depth), :], preferred_element_type=jnp.float32)
        return carry

    lax.fori_loop(0, cap, begin, 0, unroll=4)
    picked = pick_edges(d_first)
    halo[2].wait_recv()
    halo[3].wait_recv()
    turns[:, pl.ds(0, width)] = (col_own[0] - col_recv[0].astype(jnp.float32)).astype(turns.dtype)
    turns[:, pl.ds(width, width)] = (col_recv[1].astype(jnp.float32) - col_own[1]).astype(turns.dtype)
    turned = turn(picked)
    for c in range(cap):
        product = early[c] + jnp.dot(turned, wts[0, c, pl.ds(depth, width), :], preferred_element_type=jnp.float32)
        part[0, c] = product.astype(part.dtype)
    for route in range(ROUTES):
        if ORDER[0] in LEAVES[route]:
            for copy in pieces[route, ORDER[0]]:
                copy.start()

    def read_tables():
        for copy in tables:
            copy.wait_recv()
        sources = [tab_recv.at[i] for i in range(len(STEPS))] + [tab_send]
        copies = [pltpu.make_async_copy(src, tab.at[i], tab_sem.at[i]) for i, src in enumerate(sources)]
        for copy in copies:
            copy.start()
        for copy in copies:
            copy.wait()

    here = set()

    def gather(route, o, h, store):
        d = writer(o)
        k = ORDER.index(o)
        rs = pl.ds(route * height, height)
        below = children(route, o)
        plain = [v for v in below if v in LEAVES[route]]
        dense = [INNER[route].index(v) for v in below if v in INNER[route]]
        if o == (0, 0):
            dense = []
        for v in plain:
            if (route, v) not in here:
                raw[route, v].wait_recv()
                here.add((route, v))
        for i in dense:
            summed[route, INNER[route][i], h].wait_recv()
        ways = list(STEPS)

        def one(j, carry):
            t = h * share + j
            total = part[k, tab[len(ways), d, t], rs, :].astype(jnp.float32)
            for v in plain:
                slot = tab[ways.index(TREES[route][v]), d, t]
                total += raw_in[route, v][slot].astype(jnp.float32)
            for i in dense:
                total += sums_in[route, i, t].astype(jnp.float32)
            store(t, total)
            return carry

        lax.fori_loop(0, share, one, 0, unroll=8)

    def follow(route, o, h):
        if o == (0, 0):
            def store(t, total):
                out_ref[t, pl.ds(route * height, height), :] = total * 0.5

            for part_of in range(PARTS):
                gather(route, o, part_of, store)
        else:
            i = INNER[route].index(o)

            def store(t, total):
                sums[route, i, t] = total.astype(sums.dtype)

            gather(route, o, h, store)
            summed[route, o, h].start()

    def products(k, turned):
        d = writer_at(k)
        pltpu.make_async_copy(weights_ref.at[0, 0], wts.at[k, :, pl.ds(0, depth)], weight_sem.at[k]).wait()
        edge_rows(k)
        later = turn(pick_edges(writer_at(lax.rem(k + 1, len(PLAN)))))
        for c in range(cap):
            stacked = jnp.concatenate([stack(ints[0, c, d]), turned], axis=1)
            product = jnp.dot(stacked, wts[k, c], preferred_element_type=jnp.float32)
            part[k, c] = product.astype(part.dtype)

        for i, (o, sums_after) in enumerate(PLAN):
            if i == 0:
                continue
            ready = [copy for route in range(ROUTES) if o in LEAVES[route] for copy in pieces[route, o]]
            if i == len(PLAN) - 1:
                sums_after = ()
            if ready or sums_after or i == TABLES_AFTER:
                @pl.when(k == i)
                def _():
                    for copy in ready:
                        copy.start()
                    if i == TABLES_AFTER:
                        read_tables()
                    for entry in sums_after:
                        follow(*entry)
        return later

    lax.fori_loop(1, len(PLAN), products, turn(pick_edges(writer(ORDER[1]))))
    for entry in PLAN[-1][1]:
        follow(*entry)
    for route, v, h in LAST:
        rs = pl.ds(route * height, height)
        i = INNER[route].index(v)
        summed[route, v, h].wait_recv()

        def add(j, carry):
            t = h * share + j
            out_ref[t, rs, :] += sums_in[route, i, t].astype(jnp.float32) * 0.5
            return carry

        lax.fori_loop(0, share, add, 0, unroll=8)
    for copy in messages:
        copy.wait_send()


def on_device(fields, weights, src_tile, tgt_tile, counts):
    bx, rows, width = fields.shape
    _, writers, cap, depth, tile_cells = weights.shape
    tiles = 16
    height = rows // ROUTES
    leaves = sum(len(some) for some in LEAVES)
    inner = len(INNER[0])
    messages = 8 + leaves + ROUTES * inner * PARTS
    bf16 = jnp.bfloat16
    ints = jnp.concatenate(
        [jnp.swapaxes(src_tile, 1, 2), jnp.swapaxes(tgt_tile, 1, 2), counts[:, None, :]], axis=1
    )
    return pl.pallas_call(
        kernel,
        out_shape=jax.ShapeDtypeStruct((tiles, rows, tile_cells), jnp.float32),
        in_specs=[pl.BlockSpec(memory_space=pl.ANY)] * 3,
        out_specs=pl.BlockSpec(memory_space=pltpu.VMEM),
        scratch_shapes=[
            pltpu.SMEM((1, 2 * cap + 1, writers), jnp.int32),
            pltpu.VMEM((bx + 2, rows, width), jnp.float32),
            pltpu.VMEM((writers, cap, depth + width, tile_cells), bf16),
            pltpu.VMEM((writers, cap + 1, rows, tile_cells), bf16),
            pltpu.VMEM((2, rows, width), jnp.float32),
            pltpu.VMEM((2, rows, width), bf16),
            pltpu.VMEM((2, rows, width), bf16),
            pltpu.VMEM((rows, 2 * width), bf16),
            pltpu.VMEM((cap, rows, tile_cells), jnp.float32),
            pltpu.VMEM((writers, 128), jnp.int32),
            pltpu.VMEM((len(STEPS), writers, 128), jnp.int32),
            pltpu.SMEM((len(STEPS) + 1, writers, 128), jnp.int32),
            pltpu.VMEM((ROUTES, inner, tiles, height, tile_cells), bf16),
            pltpu.VMEM((ROUTES, inner, tiles, height, tile_cells), bf16),
        ]
        + [pltpu.VMEM((cap + 1, height, tile_cells), bf16)] * leaves
        + [
            pltpu.SemaphoreType.DMA((messages,)),
            pltpu.SemaphoreType.DMA((messages,)),
            pltpu.SemaphoreType.DMA((CHUNKS,)),
            pltpu.SemaphoreType.DMA((writers,)),
            pltpu.SemaphoreType.DMA((len(STEPS) + 1,)),
            pltpu.SemaphoreType.DMA,
        ],
        compiler_params=pltpu.CompilerParams(
            collective_id=0, has_side_effects=True, vmem_limit_bytes=52 * 1024 * 1024
        ),
        cost_estimate=pl.CostEstimate(flops=1208000000, bytes_accessed=19700000, transcendentals=0),
    )(ints, fields, weights)


def solution(mesh):
    placed = (
        P("face", None, "blk"),
        P(("face", "blk"), None, None, None, None),
        P(("face", "blk"), None, None),
        P(("face", "blk"), None, None),
        P(("face", "blk"), None),
    )
    return jax.shard_map(
        on_device,
        mesh=mesh,
        in_specs=placed,
        out_specs=P(("face", "blk"), None, None),
        check_vma=False,
    )
```

```python
import jax
import jax.numpy as jnp
from jax import lax
from jax.experimental import pallas as pl
from jax.experimental.pallas import tpu as pltpu
from jax.sharding import PartitionSpec as P

MESH = pl.DeviceIdType.MESH
SIDE = 4
CHUNKS = 8
ROUTES = 2
PARTS = 2
STEPS = {"x+": (1, 0), "x-": (3, 0), "y+": (0, 1), "y-": (0, 3)}
TREES = (
    {
        (0, 1): "y-", (0, 2): "y+", (0, 3): "y+", (1, 0): "x-", (1, 1): "x-",
        (1, 2): "y-", (1, 3): "x-", (2, 0): "y+", (2, 1): "x-", (2, 2): "y-",
        (2, 3): "x+", (3, 0): "x+", (3, 1): "x+", (3, 2): "y+", (3, 3): "x+",
    },
    {
        (0, 1): "y-", (0, 2): "x+", (0, 3): "y+", (1, 0): "x-", (1, 1): "y-",
        (1, 2): "y-", (1, 3): "y+", (2, 0): "x+", (2, 1): "x-", (2, 2): "x-",
        (2, 3): "x+", (3, 0): "x+", (3, 1): "y-", (3, 2): "y+", (3, 3): "y+",
    },
)
PLAN = (
    ((2, 0), ()),
    ((2, 2), ()),
    ((0, 2), ()),
    ((2, 1), ()),
    ((3, 1), ()),
    ((3, 2), ((0, (2, 1), 0), (0, (2, 1), 1),)),
    ((1, 2), ((1, (1, 2), 0), (1, (1, 2), 1),)),
    ((2, 3), ()),
    ((1, 3), ()),
    ((3, 3), ()),
    ((0, 3), ()),
    ((1, 1), (
        (0, (1, 1), 0), (0, (3, 3), 0), (1, (1, 1), 0), (0, (1, 1), 1),
        (0, (3, 3), 1),
    )),
    ((1, 0), (
        (1, (3, 3), 0), (1, (3, 3), 1), (1, (1, 1), 1),
    )),
    ((3, 0), ()),
    ((0, 1), (
        (0, (0, 1), 0), (0, (0, 3), 0), (1, (1, 0), 0),
    )),
    ((0, 0), (
        (1, (3, 0), 0), (0, (0, 1), 1), (0, (0, 3), 1), (1, (1, 0), 1),
        (1, (3, 0), 1), (0, (0, 0), 0), (1, (0, 0), 0),
    )),
)
LAST = (
    (0, (0, 3), 0), (1, (1, 0), 0), (1, (3, 0), 0), (0, (0, 1), 0),
    (0, (0, 3), 1), (1, (1, 0), 1), (1, (3, 0), 1), (0, (0, 1), 1),
)
TABLES_AFTER = 4
ORDER = tuple(entry[0] for entry in PLAN)


def parent(route, o):
    dx, dy = STEPS[TREES[route][o]]
    return ((o[0] + dx) % SIDE, (o[1] + dy) % SIDE)


def children(route, o):
    return [v for v in TREES[route] if parent(route, v) == o]


INNER = [[v for v in tree if children(route, v)] for route, tree in enumerate(TREES)]
LEAVES = [[v for v in tree if not children(route, v)] for route, tree in enumerate(TREES)]


def coded(values):
    word = sum(v << (2 * k) for k, v in enumerate(values))
    return word - (1 << 32) if word >= 1 << 31 else word


def kernel(
    ints_in, fields_ref, weights_ref, out_ref,
    ints, cells, wts, part, col_own, col_send, col_recv, turns, early, tab_send, tab_recv, tab, sums, sums_in,
    *rest,
):
    raw_in = {}
    for route in range(ROUTES):
        for v in LEAVES[route]:
            raw_in[route, v] = rest[len(raw_in)]
    send_sem, recv_sem, field_sem, weight_sem, tab_sem, ints_sem = rest[len(raw_in):]
    bx, rows, width = fields_ref.shape
    cap, writers = ints.shape[1] // 2, ints.shape[2]
    tiles = out_ref.shape[0]
    height = rows // ROUTES
    share = tiles // PARTS
    faces = lax.axis_size("face")
    face = lax.axis_index("face")
    blk = lax.axis_index("blk")
    px, py = blk // SIDE, lax.rem(blk, SIDE)

    way = 1 - 2 * lax.rem(face, 2)

    def at(a, b):
        return lax.rem(px + SIDE + way * a, SIDE) * SIDE + lax.rem(py + SIDE + way * b, SIDE)

    def writer(o):
        return at((SIDE - o[0]) % SIDE, (SIDE - o[1]) % SIDE)

    fields_in = []
    step = bx // CHUNKS
    for i in range(CHUNKS):
        copy = pltpu.make_async_copy(
            fields_ref.at[pl.ds(i * step, step)], cells.at[pl.ds(1 + i * step, step)], field_sem.at[i]
        )
        copy.start()
        fields_in.append(copy)
    near = {name: (face, at(*step)) for name, step in STEPS.items()}
    up, down = lax.rem(face + 1, faces), lax.rem(face + faces - 1, faces)
    right, left = lax.rem(blk + 1, writers), lax.rem(blk + writers - 1, writers)
    barrier = pltpu.get_barrier_semaphore()
    greeted = [(up, blk), (down, blk), (face, left), (face, right)] + list(near.values())
    for peer in greeted:
        pl.semaphore_signal(barrier, inc=1, device_id=peer, device_id_type=MESH)

    ints_copy = pltpu.make_async_copy(ints_in, ints, ints_sem)
    ints_copy.start()
    weights_in = [
        pltpu.make_async_copy(weights_ref.at[0, writer(o)], wts.at[k, :, pl.ds(0, weights_ref.shape[3])], weight_sem.at[k])
        for k, o in enumerate(ORDER)
    ]

    messages = []

    def message(src, dst, peer):
        i = len(messages)
        messages.append(
            pltpu.make_async_remote_copy(
                src_ref=src, dst_ref=dst, send_sem=send_sem.at[i], recv_sem=recv_sem.at[i],
                device_id=peer, device_id_type=MESH,
            )
        )
        return messages[i]

    halo = [
        message(fields_ref.at[bx - 1], cells.at[0], (up, blk)),
        message(fields_ref.at[0], cells.at[bx + 1], (down, blk)),
        message(col_send.at[0], col_recv.at[0], (face, right)),
        message(col_send.at[1], col_recv.at[1], (face, left)),
    ]
    tables = [message(tab_send, tab_recv.at[i], near[name]) for i, name in enumerate(STEPS)]
    raw, summed = {}, {}
    for route, tree in enumerate(TREES):
        rs = pl.ds(route * height, height)
        for v in LEAVES[route]:
            raw[route, v] = message(
                part.at[ORDER.index(v), pl.ds(0, cap), rs], raw_in[route, v].at[pl.ds(0, cap)], near[tree[v]]
            )
        for i, v in enumerate(INNER[route]):
            for h in range(PARTS):
                some = pl.ds(h * share, share)
                summed[route, v, h] = message(sums.at[route, i, some], sums_in.at[route, i, some], near[tree[v]])

    depth = weights_ref.shape[3]
    group = width // cap

    def clear(k, carry):
        for c in range(cap):
            wts[k, c, pl.ds(depth, width), :] = jnp.zeros((width, wts.shape[3]), wts.dtype)
        return carry

    lax.fori_loop(0, writers, clear, 0)

    lanes = lax.broadcasted_iota(jnp.int32, (rows, width), 1)

    def pack_edges():
        edges = (jnp.zeros((rows, width), jnp.float32), jnp.zeros((rows, width), jnp.float32))
        for i in range(CHUNKS):
            fields_in[i].wait()
            if i >= CHUNKS // 2:
                weights_in[i - CHUNKS // 2].start()

            def pick(j, edges):
                x = i * step + j
                turned = pltpu.roll(cells[1 + x], lax.rem(x + 1, width), 1)
                return (
                    jnp.where(lanes == x, turned, edges[0]),
                    jnp.where(lanes == lax.rem(x + 1, width), turned, edges[1]),
                )

            edges = lax.fori_loop(0, step, pick, edges, unroll=4)
        for i in range(2):
            col_own[i] = edges[i]
            col_send[i] = edges[i].astype(col_send.dtype)

    core = lax.rem(face, 2)
    pl.when(core == 0)(pack_edges)
    pl.semaphore_wait(barrier, len(greeted))
    halo[0].start()
    halo[1].start()
    pl.when(core != 0)(pack_edges)
    halo[2].start()
    halo[3].start()
    for copy in weights_in[CHUNKS - CHUNKS // 2:]:
        copy.start()

    ints_copy.wait()
    lane = lax.broadcasted_iota(jnp.int32, (1, 128), 1)

    def make_row(d, carry):
        row = jnp.full((1, 128), cap, jnp.int32)
        for c in range(cap):
            target = jnp.where(c < ints[0, 2 * cap, d], ints[0, cap + c, d], 127)
            row = jnp.where(lane == target, c, row)
        tab_send[pl.ds(d, 1), :] = row
        return carry

    lax.fori_loop(0, writers, make_row, 0)
    for copy in tables:
        copy.start()
    for buf in raw_in.values():
        buf[cap] = jnp.zeros((height, width), buf.dtype)
    for k, o in enumerate(ORDER):
        if o not in LEAVES[0] or o not in LEAVES[1]:
            part[k, cap] = jnp.zeros((rows, width), part.dtype)
    group_row = lax.broadcasted_iota(jnp.int32, (group, wts.shape[3]), 0)
    turn_row = lax.broadcasted_iota(jnp.int32, (2 * width, width), 0)
    code_x = jnp.int32(coded([(SIDE - o[0]) % SIDE for o in ORDER]))
    code_y = jnp.int32(coded([(SIDE - o[1]) % SIDE for o in ORDER]))

    def writer_at(k):
        return at((code_x >> (2 * k)) & 3, (code_y >> (2 * k)) & 3)

    def stack(x):
        value = cells[x + 1]
        grad_x = cells[x + 2] - cells[x]
        grad_y = pltpu.roll(value, width - 1, 1) - pltpu.roll(value, 1, 1)
        return jnp.concatenate([value + value, grad_x, grad_y], axis=1).astype(jnp.bfloat16)

    def pick_edges(d):
        where_from = jnp.full((1, width), -1, jnp.int32)
        for c in range(cap):
            x = ints[0, c, d]
            where_from = jnp.where(lane == c * group, x, where_from)
            where_from = jnp.where(lane == c * group + group - 1, width + lax.rem(x + 1, width), where_from)
        return jnp.where(turn_row == where_from, 1.0, 0.0).astype(jnp.bfloat16)

    def turn(picked):
        return jnp.dot(turns[...], picked, preferred_element_type=jnp.float32).astype(jnp.bfloat16)

    def edge_rows(k):
        for c in range(cap):
            first = wts[k, c, pl.ds(2 * width, group), :].astype(jnp.float32)
            final = wts[k, c, pl.ds(3 * width - group, group), :].astype(jnp.float32)
            edge = jnp.where(group_row == 0, first, jnp.where(group_row == group - 1, final, 0.0))
            wts[k, c, pl.ds(depth + c * group, group), :] = edge.astype(wts.dtype)

    halo[0].wait_recv()
    halo[1].wait_recv()
    weights_in[0].wait()
    edge_rows(0)
    d_first = writer(ORDER[0])

    def begin(c, carry):
        early[c] = jnp.dot(stack(ints[0, c, d_first]), wts[0, c, pl.ds(0, depth), :], preferred_element_type=jnp.float32)
        return carry

    lax.fori_loop(0, cap, begin, 0, unroll=4)
    picked = pick_edges(d_first)
    halo[2].wait_recv()
    halo[3].wait_recv()
    turns[:, pl.ds(0, width)] = (col_own[0] - col_recv[0].astype(jnp.float32)).astype(turns.dtype)
    turns[:, pl.ds(width, width)] = (col_recv[1].astype(jnp.float32) - col_own[1]).astype(turns.dtype)
    turned = turn(picked)
    for c in range(cap):
        product = early[c] + jnp.dot(turned, wts[0, c, pl.ds(depth, width), :], preferred_element_type=jnp.float32)
        part[0, c] = product.astype(part.dtype)
    for route in range(ROUTES):
        if ORDER[0] in LEAVES[route]:
            raw[route, ORDER[0]].start()

    def read_tables():
        for copy in tables:
            copy.wait_recv()
        sources = [tab_recv.at[i] for i in range(len(STEPS))] + [tab_send]
        copies = [pltpu.make_async_copy(src, tab.at[i], tab_sem.at[i]) for i, src in enumerate(sources)]
        for copy in copies:
            copy.start()
        for copy in copies:
            copy.wait()

    here = set()

    def gather(route, o, h, store):
        d = writer(o)
        k = ORDER.index(o)
        rs = pl.ds(route * height, height)
        below = children(route, o)
        plain = [v for v in below if v in LEAVES[route]]
        dense = [INNER[route].index(v) for v in below if v in INNER[route]]
        if o == (0, 0):
            dense = []
        for v in plain:
            if (route, v) not in here:
                raw[route, v].wait_recv()
                here.add((route, v))
        for i in dense:
            summed[route, INNER[route][i], h].wait_recv()
        ways = list(STEPS)

        def one(j, carry):
            t = h * share + j
            total = part[k, tab[len(ways), d, t], rs, :].astype(jnp.float32)
            for v in plain:
                slot = tab[ways.index(TREES[route][v]), d, t]
                total += raw_in[route, v][slot].astype(jnp.float32)
            for i in dense:
                total += sums_in[route, i, t].astype(jnp.float32)
            store(t, total)
            return carry

        lax.fori_loop(0, share, one, 0, unroll=8)

    def follow(route, o, h):
        if o == (0, 0):
            def store(t, total):
                out_ref[t, pl.ds(route * height, height), :] = total * 0.5

            for part_of in range(PARTS):
                gather(route, o, part_of, store)
        else:
            i = INNER[route].index(o)

            def store(t, total):
                sums[route, i, t] = total.astype(sums.dtype)

            gather(route, o, h, store)
            summed[route, o, h].start()

    def products(k, turned):
        d = writer_at(k)
        pltpu.make_async_copy(weights_ref.at[0, 0], wts.at[k, :, pl.ds(0, depth)], weight_sem.at[k]).wait()
        edge_rows(k)
        later = turn(pick_edges(writer_at(lax.rem(k + 1, len(PLAN)))))
        for c in range(cap):
            stacked = jnp.concatenate([stack(ints[0, c, d]), turned], axis=1)
            product = jnp.dot(stacked, wts[k, c], preferred_element_type=jnp.float32)
            part[k, c] = product.astype(part.dtype)

        for i, (o, sums_after) in enumerate(PLAN):
            if i == 0:
                continue
            ready = [raw[route, o] for route in range(ROUTES) if o in LEAVES[route]]
            if i == len(PLAN) - 1:
                sums_after = ()
            if ready or sums_after or i == TABLES_AFTER:
                @pl.when(k == i)
                def _():
                    for copy in ready:
                        copy.start()
                    if i == TABLES_AFTER:
                        read_tables()
                    for entry in sums_after:
                        follow(*entry)
        return later

    lax.fori_loop(1, len(PLAN), products, turn(pick_edges(writer(ORDER[1]))))
    for entry in PLAN[-1][1]:
        follow(*entry)
    for route, v, h in LAST:
        rs = pl.ds(route * height, height)
        i = INNER[route].index(v)
        summed[route, v, h].wait_recv()

        def add(j, carry):
            t = h * share + j
            out_ref[t, rs, :] += sums_in[route, i, t].astype(jnp.float32) * 0.5
            return carry

        lax.fori_loop(0, share, add, 0, unroll=8)
    for copy in messages:
        copy.wait_send()


def on_device(fields, weights, src_tile, tgt_tile, counts):
    bx, rows, width = fields.shape
    _, writers, cap, depth, tile_cells = weights.shape
    tiles = 16
    height = rows // ROUTES
    leaves = sum(len(some) for some in LEAVES)
    inner = len(INNER[0])
    messages = 8 + leaves + ROUTES * inner * PARTS
    bf16 = jnp.bfloat16
    ints = jnp.concatenate(
        [jnp.swapaxes(src_tile, 1, 2), jnp.swapaxes(tgt_tile, 1, 2), counts[:, None, :]], axis=1
    )
    return pl.pallas_call(
        kernel,
        out_shape=jax.ShapeDtypeStruct((tiles, rows, tile_cells), jnp.float32),
        in_specs=[pl.BlockSpec(memory_space=pl.ANY)] * 3,
        out_specs=pl.BlockSpec(memory_space=pltpu.VMEM),
        scratch_shapes=[
            pltpu.SMEM((1, 2 * cap + 1, writers), jnp.int32),
            pltpu.VMEM((bx + 2, rows, width), jnp.float32),
            pltpu.VMEM((writers, cap, depth + width, tile_cells), bf16),
            pltpu.VMEM((writers, cap + 1, rows, tile_cells), bf16),
            pltpu.VMEM((2, rows, width), jnp.float32),
            pltpu.VMEM((2, rows, width), bf16),
            pltpu.VMEM((2, rows, width), bf16),
            pltpu.VMEM((rows, 2 * width), bf16),
            pltpu.VMEM((cap, rows, tile_cells), jnp.float32),
            pltpu.VMEM((writers, 128), jnp.int32),
            pltpu.VMEM((len(STEPS), writers, 128), jnp.int32),
            pltpu.SMEM((len(STEPS) + 1, writers, 128), jnp.int32),
            pltpu.VMEM((ROUTES, inner, tiles, height, tile_cells), bf16),
            pltpu.VMEM((ROUTES, inner, tiles, height, tile_cells), bf16),
        ]
        + [pltpu.VMEM((cap + 1, height, tile_cells), bf16)] * leaves
        + [
            pltpu.SemaphoreType.DMA((messages,)),
            pltpu.SemaphoreType.DMA((messages,)),
            pltpu.SemaphoreType.DMA((CHUNKS,)),
            pltpu.SemaphoreType.DMA((writers,)),
            pltpu.SemaphoreType.DMA((len(STEPS) + 1,)),
            pltpu.SemaphoreType.DMA,
        ],
        compiler_params=pltpu.CompilerParams(
            collective_id=0, has_side_effects=True, vmem_limit_bytes=52 * 1024 * 1024
        ),
        cost_estimate=pl.CostEstimate(flops=1208000000, bytes_accessed=19700000, transcendentals=0),
    )(ints, fields, weights)


def solution(mesh):
    placed = (
        P("face", None, "blk"),
        P(("face", "blk"), None, None, None, None),
        P(("face", "blk"), None, None),
        P(("face", "blk"), None, None),
        P(("face", "blk"), None),
    )
    return jax.shard_map(
        on_device,
        mesh=mesh,
        in_specs=placed,
        out_specs=P(("face", "blk"), None, None),
        check_vma=False,
    )
```
